32 devices in a mesh: seq: 8 (over z, y), tp: 4 (over x, core).
Axes of the slice: x: 2, y: 2, z: 4, core: 2. Of those that a mesh axis runs over, the one named last changes fastest.
Arguments:
- tokens: bfloat16 [2, 2, 2048, 1024], P(None, None, 'seq'), may hold values from -6 to 6
- lengths: int32 [2, 2], replicated, may hold values from 256 to 2048, as said below
- norm1_gain: float32 [1024], replicated, may hold values from 0.1 to 1.9
- in_weight: bfloat16 [1024, 3072], replicated, may hold values from -0.1875 to 0.1875
- conv_weight: bfloat16 [3, 1024], replicated, may hold values from -3.5 to 3.5
- out_weight: bfloat16 [1024, 1024], replicated, may hold values from -0.1875 to 0.1875
- norm2_gain: float32 [1024], replicated, may hold values from 0.1 to 1.9
- gate_weight: bfloat16 [1024, 4608], P(None, 'tp'), may hold values from -0.1875 to 0.1875
- up_weight: bfloat16 [1024, 4608], P(None, 'tp'), may hold values from -0.1875 to 0.1875
- down_weight: bfloat16 [4608, 1024], P('tp'), may hold values from -0.09375 to 0.09375
- cotangent: bfloat16 [2, 2, 2048, 1024], P(None, None, 'seq'), may hold values from -6 to 6
Outputs:
- mixed: bfloat16 [2, 2, 2048, 1024], P(None, None, 'seq')
- tokens_grad: bfloat16 [2, 2, 2048, 1024], P(None, None, 'seq')
- grad_norm1: float32 [1024], P('seq')
- grad_in: float32 [1024, 3072], P('seq', 'tp')
- grad_conv: float32 [3, 1024], P(None, 'seq')
- grad_out: float32 [1024, 1024], P('seq', 'tp')
- grad_norm2: float32 [1024], P('seq')
- grad_gate: float32 [1024, 4608], P('seq', 'tp')
- grad_up: float32 [1024, 4608], P('seq', 'tp')
- grad_down: float32 [4608, 1024], P('tp', 'seq')
The draws below stay inside these ranges and needn't reach their ends.
Inputs may be any that keep to these rules, and one draw needn't show every extreme that they name: `lengths`: in every micro-batch one of the 2 sequences, which one varies, holds all 2048 positions; positions at or past a sequence's length are padding.
All inputs are finite; a program needn't handle non-finite values.
Results may differ from the reference program's by a relative error of at most 0.011.
Values may be sent and summed in bfloat16 or wider, within the bound.
No kernel may reach another device: no remote copies, remote signals or barrier semaphores. Data moves between devices by JAX's collectives and lax.ppermute only.
A program may use at most 192 MiB of HBM per device.

```python
import jax
import jax.numpy as jnp
from jax import lax

D = 1024
FF = 4608
KERNEL = 3
LEN_DEV = 256
SEQS = 2
MICRO = 2
LENGTH = 2048


def draw_lengths(key, part):
    key = jax.random.fold_in(key, 11)
    pick_key, length_key = jax.random.split(key)
    full_seq = jax.random.randint(pick_key, (MICRO, 1), 0, SEQS)
    drawn_lengths = jax.random.randint(length_key, (MICRO, SEQS), LEN_DEV, LENGTH + 1)
    full_flag = jnp.arange(SEQS, dtype=jnp.int32)[None, :] == full_seq
    return jnp.where(full_flag, LENGTH, drawn_lengths).astype(jnp.int32)


def levels(rng, dims, pieces, smallest, top_value):
    factor_of = 1.0
    for position, shards_of in pieces:
        steps = jax.random.uniform(jax.random.fold_in(jax.random.fold_in(rng, 6), position), (shards_of,), jnp.float32, smallest / len(pieces), top_value / len(pieces))
        factor_of = factor_of * jnp.repeat(jnp.exp(steps), dims[position] // shards_of).reshape((-1,) + (1,) * (len(dims) - 1 - position))
    return factor_of


def gaussian(key, extent, deviation, reach, cuts=(), kind=jnp.bfloat16):
    entries = jax.random.normal(key, extent, jnp.float32) * deviation
    if len(cuts) > 0:
        entries = levels(key, extent, cuts, -0.22, 0.18) * entries
    return jnp.clip(entries, min=-reach, max=reach).astype(kind)


def setup_inputs(seed: int = 0) -> dict:
    key_list = jax.random.split(jax.random.key(seed), 12)
    return {
        "tokens": gaussian(key_list[0], (MICRO, SEQS, LENGTH, D), 1.0, 6.0, ((2, 8),)),
        "lengths": draw_lengths(jax.random.fold_in(key_list[11], 71), 0),
        "norm1_gain": jnp.clip(1.0 + 0.18 * jax.random.normal(key_list[2], (D,), jnp.float32), 0.1, 1.9),
        "in_weight": gaussian(key_list[3], (D, 3 * D), D ** -0.5, 0.1875),
        "conv_weight": gaussian(key_list[4], (KERNEL, D), KERNEL ** -0.5, 3.5),
        "out_weight": gaussian(key_list[5], (D, D), D ** -0.5, 0.1875),
        "norm2_gain": jnp.clip(1.0 + 0.18 * jax.random.normal(key_list[6], (D,), jnp.float32), 0.1, 1.9),
        "gate_weight": gaussian(key_list[7], (D, FF), D ** -0.5, 0.1875, ((1, 4),)),
        "up_weight": gaussian(key_list[8], (D, FF), D ** -0.5, 0.1875, ((1, 4),)),
        "down_weight": gaussian(key_list[9], (FF, D), FF ** -0.5, 0.09375, ((0, 4),)),
        "cotangent": gaussian(key_list[10], (MICRO, SEQS, LENGTH, D), 1.0, 6.0, ((2, 8),)),
    }


eps = 1e-05

@jax.custom_vjp
def low(v):
    return lax.optimization_barrier(v.astype(jnp.bfloat16)).astype(jnp.float32)

@jax.custom_vjp
def low_back(v):
    return v

def low_keep(v):
    return (low(v), None)

def low_pass(kept, grad):
    return (grad,)

def back_keep(v):
    return (v, None)

def back_low(kept, grad):
    return (low(grad),)
low.defvjp(low_keep, low_pass)
low_back.defvjp(back_keep, back_low)

def precise_dot(left, right):
    return jnp.dot(left, right, precision=lax.Precision.HIGHEST, preferred_element_type=jnp.float32)

def block_forward(inputs, norm_one, weight_in, conv_taps, weight_out, norm_two, weight_gate, weight_up, weight_down, token_mask):
    model_width = inputs.shape[1]
    seq_positions = inputs.shape[0]
    scale_one = lax.rsqrt(lax.optimization_barrier(jnp.mean(inputs * inputs, axis=-1, keepdims=True)) + eps)
    normed_one = low(inputs * scale_one * norm_one)
    projected = low_back(precise_dot(normed_one, weight_in))
    b_part = projected[:, :model_width]
    c_part = projected[:, model_width:2 * model_width]
    x_part = projected[:, 2 * model_width:]
    product = low(b_part * x_part)
    padded = jnp.pad(product, ((2, 0), (0, 0)))
    conv_out = low_back(conv_taps[0] * padded[0:seq_positions] + conv_taps[1] * padded[1:seq_positions + 1] + conv_taps[2] * padded[2:seq_positions + 2])
    gated_out = low(c_part * conv_out)
    residual = inputs + low_back(precise_dot(gated_out, weight_out))
    scale_two = lax.rsqrt(lax.optimization_barrier(jnp.mean(residual * residual, axis=-1, keepdims=True)) + eps)
    normed_two = low(residual * scale_two * norm_two)
    gate_proj = low_back(precise_dot(normed_two, weight_gate))
    up_proj = low_back(precise_dot(normed_two, weight_up))
    activated = low(jax.nn.silu(gate_proj) * up_proj)
    ffn_out = low_back(precise_dot(activated, weight_down))
    return token_mask * (residual + ffn_out)

def reference(tokens, lengths, norm1_gain, in_weight, conv_weight, out_weight, norm2_gain, gate_weight, up_weight, down_weight, cotangent):
    params = tuple((array_in.astype(jnp.float32) for array_in in (norm1_gain, in_weight, conv_weight, out_weight, norm2_gain, gate_weight, up_weight, down_weight)))
    seq_tokens = tokens.reshape(MICRO * SEQS, LENGTH, D)
    seq_cotangent = cotangent.reshape(MICRO * SEQS, LENGTH, D)
    seq_lengths = lengths.reshape(MICRO * SEQS).astype(jnp.int32)
    positions = jnp.arange(LENGTH, dtype=jnp.int32)

    def one_sequence(running, seq_items):
        inputs, seq_cot, seq_length = seq_items
        token_mask = (positions < seq_length).astype(jnp.float32)[:, None]

        def forward(inputs_wide, *weights_wide):
            return block_forward(inputs_wide, *weights_wide, token_mask)
        output, pullback = jax.vjp(forward, inputs.astype(jnp.float32), *params)
        all_grads = pullback(seq_cot.astype(jnp.float32))
        running = tuple((total + piece for total, piece in zip(running, all_grads[1:])))
        return (running, (output.astype(jnp.bfloat16), all_grads[0].astype(jnp.bfloat16)))
    initial = tuple((jnp.zeros(array_in.shape, jnp.float32) for array_in in params))
    totals, (outputs, input_grads) = lax.scan(one_sequence, initial, (seq_tokens, seq_cotangent, seq_lengths))
    return (outputs.reshape(tokens.shape), input_grads.reshape(tokens.shape), totals[0], totals[1], totals[2], totals[3], totals[4], totals[5], totals[6], totals[7])
```

```python
import jax
import jax.numpy as jnp
from jax import lax
from jax.sharding import PartitionSpec as P

eps = 1e-05
wide = jnp.float32
low = jnp.bfloat16


def shift_blocks(block, distance):
    devices = range(lax.axis_size("seq"))
    route = [(i - distance, i) for i in devices if i - distance in devices]
    return lax.ppermute(block, "seq", route)


def swap(block, axis, mask):
    return lax.ppermute(block, axis, [(i, i ^ mask) for i in range(lax.axis_size(axis))])


def matmul(left, right):
    return jnp.dot(left, right, preferred_element_type=wide)


def matmul_nt(left, right):
    return lax.dot_general(left, right, (((1,), (1,)), ((), ())), preferred_element_type=wide)


def matmul_tn(left, right):
    return lax.dot_general(left, right, (((0,), (0,)), ((), ())), preferred_element_type=wide)


def pick(array, axis, index):
    return lax.dynamic_index_in_dim(array, index, axis, keepdims=False)


class Spread:
    def __init__(self, masks):
        self.masks = masks
        self.count = lax.axis_size("seq")
        self.index = lax.axis_index("seq")

    def bit(self, mask):
        return (self.index // mask) % 2

    def split_columns(self, array):
        mask = self.masks[0]
        rows, width = array.shape
        share = width // self.count
        view = array.reshape(rows, self.count // (2 * mask), 2, mask * share)
        mine = self.bit(mask)
        send = pick(view, 2, 1 - mine).reshape(rows, width // 2)
        keep = pick(view, 2, mine).reshape(rows, width // 2)
        return send, keep

    def finish(self, send, keep):
        left = [m for m in sorted(self.masks, reverse=True) if m != self.masks[0]]
        share = 2 * send.shape[0] // self.count
        total = keep + swap(send.astype(low), "seq", self.masks[0]).astype(wide)
        total = total.reshape((2,) * len(left) + (share, send.shape[1]))
        for mask in self.masks[1:]:
            place = left.index(mask)
            left.pop(place)
            mine = self.bit(mask)
            send = pick(total, place, 1 - mine).astype(low)
            keep = pick(total, place, mine)
            total = keep + swap(send, "seq", mask).astype(wide)
        return total


def spread_vectors(vectors):
    count, index = lax.axis_size("seq"), lax.axis_index("seq")
    mask = count // 2
    total = vectors
    while mask:
        mine = (index // mask) % 2
        view = total.reshape((2, mask) + total.shape[1:])
        total = pick(view, 0, mine) + swap(pick(view, 0, 1 - mine), "seq", mask)
        mask //= 2
    return total.reshape(total.shape[1:])


def sum_over_x(block):
    count = lax.axis_size("tp")
    total = block
    mask = 2
    while mask < count:
        total = total.astype(low)
        total = total.astype(wide) + swap(total, "tp", mask).astype(wide)
        mask *= 2
    return total


def body(
    tokens,
    lengths,
    norm1_gain,
    in_weight,
    conv_weight,
    out_weight,
    norm2_gain,
    gate_weight,
    up_weight,
    down_weight,
    cotangent,
):
    micro_count, seq_count, shard_length, width = tokens.shape
    tp_count, tp_index = lax.axis_size("tp"), lax.axis_index("tp")
    seq_total, seq_index = lax.axis_size("seq"), lax.axis_index("seq")
    core = tp_index % 2
    own_micro = micro_count // 2
    rows = own_micro * seq_count * shard_length
    groups = own_micro * seq_count
    in_share = in_weight.shape[1] // tp_count
    out_share = width // tp_count
    share = width // seq_total
    masks = []
    mask = 1
    while mask < seq_total:
        masks.append(mask)
        mask *= 2
    spread = Spread(masks)
    taps = conv_weight.astype(wide)
    positions = seq_index * shard_length + jnp.arange(shard_length, dtype=jnp.int32)

    def micro_half(array, which):
        return lax.dynamic_slice_in_dim(array, which * own_micro, own_micro, 0)

    def row_mask(which):
        half = micro_half(lengths, which)
        return (positions[None, None, :] < half[:, :, None]).astype(wide).reshape(rows, 1)

    def both_cores(own):
        other = swap(own, "tp", 1)
        own = own.reshape(own_micro, seq_count, shard_length, width)
        other = other.reshape(own_micro, seq_count, shard_length, width)
        return jnp.where(
            core == 0,
            jnp.concatenate([own, other], axis=0),
            jnp.concatenate([other, own], axis=0),
        )

    inputs = micro_half(tokens, core).astype(wide).reshape(rows, width)
    scale_one = lax.rsqrt(jnp.mean(inputs * inputs, axis=-1, keepdims=True) + eps)
    normed_one_f = inputs * scale_one
    normed_one = (normed_one_f * norm1_gain).astype(low)
    b_part = matmul(normed_one, in_weight[:, :width])
    x_part = matmul(normed_one, in_weight[:, 2 * width :])
    product = (b_part * x_part).astype(low).reshape(groups, shard_length, width)
    before = shift_blocks(product[:, shard_length - 2 :], 1)
    c_part = matmul(normed_one, in_weight[:, width : 2 * width])
    extended = jnp.concatenate([before, product], axis=1).astype(wide)
    conv_out = (
        taps[0] * extended[:, 0:shard_length]
        + taps[1] * extended[:, 1 : shard_length + 1]
        + taps[2] * extended[:, 2 : shard_length + 2]
    ).reshape(rows, width)
    gated_out = (c_part * conv_out).astype(low)
    residual = inputs + matmul(gated_out, out_weight)
    scale_two = lax.rsqrt(jnp.mean(residual * residual, axis=-1, keepdims=True) + eps)
    normed_two_f = residual * scale_two
    normed_own = (normed_two_f * norm2_gain).astype(low)
    normed_other = swap(normed_own, "tp", 1)

    own_mask = row_mask(core)
    out_grad = micro_half(cotangent, core).astype(wide).reshape(rows, width) * own_mask
    other_grad = micro_half(cotangent, 1 - core).astype(wide).reshape(rows, width) * row_mask(
        1 - core
    )
    halves = []
    for normed, grad in ((normed_own, out_grad), (normed_other, other_grad)):
        out_low = grad.astype(low)
        gate_proj = matmul(normed, gate_weight)
        up_proj = matmul(normed, up_weight)
        sigmoid_gate = jax.nn.sigmoid(gate_proj)
        silu_gate = gate_proj * sigmoid_gate
        activated = (silu_gate * up_proj).astype(low)
        act_grad = matmul_nt(out_low, down_weight)
        gate_grad = (
            act_grad * up_proj * sigmoid_gate * (1.0 + gate_proj * (1.0 - sigmoid_gate))
        ).astype(low)
        up_grad = (act_grad * silu_gate).astype(low)
        two_terms = matmul_nt(gate_grad, gate_weight) + matmul_nt(up_grad, up_weight)
        ffn_terms = matmul(activated, down_weight)
        halves.append((normed, out_low, activated, gate_grad, up_grad, two_terms, ffn_terms))
    normed_all, out_all, activated_all, gate_all, up_all = (
        jnp.concatenate([halves[0][i], halves[1][i]], axis=0) for i in range(5)
    )
    out_send, out_keep = spread.split_columns(out_all)
    normed_send, normed_keep = spread.split_columns(normed_all)
    grad_down = spread.finish(
        matmul_tn(out_send, activated_all), matmul_tn(out_keep, activated_all)
    ).T
    grad_gate = spread.finish(matmul_tn(normed_send, gate_all), matmul_tn(normed_keep, gate_all))
    grad_up = spread.finish(matmul_tn(normed_send, up_all), matmul_tn(normed_keep, up_all))

    two_sum = halves[0][5] + swap(halves[1][5].astype(low), "tp", 1).astype(wide)
    norm_two_grad = sum_over_x(two_sum)
    ffn_sum = halves[0][6] + swap(halves[1][6].astype(low), "tp", 1).astype(wide)
    ffn_out = sum_over_x(ffn_sum)
    mixed = both_cores(((residual + ffn_out) * own_mask).astype(low))

    grad_norm2 = jnp.sum(norm_two_grad * normed_two_f, axis=0)
    weighted_two = norm_two_grad * norm2_gain
    residual_grad = out_grad + scale_two * (
        weighted_two - normed_two_f * jnp.mean(weighted_two * normed_two_f, axis=-1, keepdims=True)
    )
    residual_low = residual_grad.astype(low)
    gated_grad = matmul_nt(residual_low, out_weight)
    conv_grad = (gated_grad * c_part).astype(low).reshape(groups, shard_length, width)
    after = shift_blocks(conv_grad[:, :2], -1)
    ext_back = jnp.concatenate([conv_grad, after], axis=1).astype(wide)
    conv_grad_wide = ext_back[:, :shard_length]
    grad_conv = jnp.stack(
        [
            jnp.sum(conv_grad_wide * extended[:, offset : offset + shard_length], axis=(0, 1))
            for offset in range(taps.shape[0])
        ]
    )
    product_grad = (
        taps[0] * ext_back[:, 2 : shard_length + 2]
        + taps[1] * ext_back[:, 1 : shard_length + 1]
        + taps[2] * ext_back[:, 0:shard_length]
    ).reshape(rows, width)
    projected_grad = jnp.concatenate(
        [product_grad * x_part, gated_grad * conv_out, product_grad * b_part], axis=-1
    ).astype(low)

    def tp_columns(array, columns, index):
        return lax.dynamic_slice_in_dim(array, index * columns, columns, 1)

    peer = tp_index + 1 - 2 * core

    def over_cores(left, right, columns):
        sent = swap(matmul_tn(left, tp_columns(right, columns, peer)).astype(low), "tp", 1)
        return matmul_tn(left, tp_columns(right, columns, tp_index)) + sent.astype(wide)

    out_local = over_cores(gated_out, residual_low, out_share)
    in_local = over_cores(normed_one, projected_grad, in_share)
    tail = jnp.concatenate([in_local, out_local], axis=1)
    mine = spread.bit(masks[0])
    view = tail.reshape(seq_total // 2, 2, share, tail.shape[1])
    tail = spread.finish(
        pick(view, 1, 1 - mine).reshape(width // 2, -1), pick(view, 1, mine).reshape(width // 2, -1)
    )
    grad_in, grad_out = tail[:, :in_share], tail[:, in_share:]

    norm_one_grad = matmul_nt(projected_grad, in_weight)
    grad_norm1 = jnp.sum(norm_one_grad * normed_one_f, axis=0)
    weighted_one = norm_one_grad * norm1_gain
    input_grad = residual_grad + scale_one * (
        weighted_one - normed_one_f * jnp.mean(weighted_one * normed_one_f, axis=-1, keepdims=True)
    )
    tokens_grad = both_cores(input_grad.astype(low))

    vectors = jnp.concatenate([grad_norm1[None], grad_norm2[None], grad_conv], axis=0)
    vectors = vectors + swap(vectors, "tp", 1)
    vectors = spread_vectors(vectors.reshape(-1, seq_total, share).transpose(1, 0, 2))
    return (
        mixed,
        tokens_grad,
        vectors[0],
        grad_in,
        vectors[2:],
        grad_out,
        vectors[1],
        grad_gate,
        grad_up,
        grad_down,
    )


def solution(mesh):
    placed = (
        P(None, None, "seq", None),
        P(),
        P(),
        P(),
        P(),
        P(),
        P(),
        P(None, "tp"),
        P(None, "tp"),
        P("tp", None),
        P(None, None, "seq", None),
    )
    return jax.shard_map(
        body,
        mesh=mesh,
        in_specs=placed,
        out_specs=(
            P(None, None, "seq", None),
            P(None, None, "seq", None),
            P("seq"),
            P("seq", "tp"),
            P(None, "seq"),
            P("seq", "tp"),
            P("seq"),
            P("seq", "tp"),
            P("seq", "tp"),
            P("tp", "seq"),
        ),
        check_vma=False,
    )
```

```python
import functools

import jax
import jax.numpy as jnp
from jax import lax
from jax.experimental import pallas as pl
from jax.experimental.pallas import tpu as pltpu
from jax.sharding import PartitionSpec as P

eps = 1e-05
wide = jnp.float32
low = jnp.bfloat16


def shift_blocks(block, distance):
    devices = range(lax.axis_size("seq"))
    route = [(i - distance, i) for i in devices if i - distance in devices]
    return lax.ppermute(block, "seq", route)


def swap(block, axis, mask):
    return lax.ppermute(block, axis, [(i, i ^ mask) for i in range(lax.axis_size(axis))])


def matmul(left, right):
    return jnp.dot(left, right, preferred_element_type=wide)


def matmul_nt(left, right):
    return lax.dot_general(left, right, (((1,), (1,)), ((), ())), preferred_element_type=wide)


def matmul_tn(left, right):
    return lax.dot_general(left, right, (((0,), (0,)), ((), ())), preferred_element_type=wide)


def pick(array, axis, index):
    return lax.dynamic_index_in_dim(array, index, axis, keepdims=False)


lanes = 128


def grad_kernel(blocks, pairs, has_add, select, *refs):
    del select
    out = refs[-1]
    add = refs[-2] if has_add else None
    start = 0
    refs = list(refs)
    for group in pairs:
        total = None
        for _ in range(group):
            lefts = [refs.pop(0)[...] for _ in range(blocks)]
            left = lefts[0] if blocks == 1 else jnp.concatenate(lefts, axis=1)
            term = matmul_tn(left, refs.pop(0)[...])
            total = term if total is None else total + term
        stop = start + total.shape[1]
        if has_add:
            total = total + add[:, start:stop].astype(wide)
        out[:, start:stop] = total.astype(out.dtype)
        start = stop


def weight_grad(groups, shares, columns, bit, mask, block, add=None):
    width = groups[0][0][0].shape[1]
    run = mask * block
    unit = run if run % lanes == 0 else width // 2
    count = width // 2 // unit
    select = jnp.stack([bit, columns]).astype(jnp.int32)
    operands, specs = [], []

    def left_map(k):
        return lambda i, chosen: (0, 2 * k + chosen[0])

    for group, share in zip(groups, shares):
        for left, right in group:
            rows = left.shape[0]
            if run % lanes:
                view = left.reshape(rows, width // (2 * run), 2, run)
                picked = lax.dynamic_index_in_dim(view, bit, 2, keepdims=False)
                operands.append(picked.reshape(rows, width // 2))
                specs.append(pl.BlockSpec((rows, width // 2), lambda i, chosen: (0, 0)))
            else:
                for k in range(count):
                    operands.append(left)
                    specs.append(pl.BlockSpec((rows, unit), left_map(k)))
            operands.append(right)
            specs.append(pl.BlockSpec((rows, share), lambda i, chosen: (0, chosen[1])))
    total = sum(shares)
    if add is not None:
        operands.append(add)
        specs.append(pl.BlockSpec((width // 2, total), lambda i, chosen: (0, 0)))
    return pl.pallas_call(
        functools.partial(grad_kernel, count, tuple(len(g) for g in groups), add is not None),
        grid_spec=pltpu.PrefetchScalarGridSpec(
            num_scalar_prefetch=1,
            grid=(1,),
            in_specs=specs,
            out_specs=pl.BlockSpec((width // 2, total), lambda i, chosen: (0, 0)),
        ),
        out_shape=jax.ShapeDtypeStruct((width // 2, total), low),
        compiler_params=pltpu.CompilerParams(vmem_limit_bytes=40 * 2**20),
        cost_estimate=pl.CostEstimate(
            flops=sum(width * share * p[0].shape[0] for g, share in zip(groups, shares) for p in g),
            bytes_accessed=8 * 2**20,
            transcendentals=0,
        ),
    )(select, *operands)


class Order:
    def __init__(self):
        self.last = None

    def __call__(self, task, *values):
        if self.last is not None:
            values, _ = lax.optimization_barrier((values, self.last))
        result = task(*values)
        self.last = result
        return result


class Spread:
    def __init__(self, masks, share):
        self.masks = masks
        self.share = share
        self.count = lax.axis_size("seq")
        self.index = lax.axis_index("seq")

    def bit(self, mask):
        return (self.index // mask) % 2

    def local(self, groups, shares, columns, kept, add=None):
        mask = self.masks[0]
        mine = self.bit(mask)
        bit = mine if kept else 1 - mine
        return weight_grad(groups, shares, columns, bit, mask, self.share, add)

    def left(self, step):
        gone = self.masks[: step + 1]
        return [m for m in sorted(self.masks, reverse=True) if m not in gone]

    def join(self, step, keep, received):
        total = keep.astype(wide) + received.astype(wide)
        left = self.left(step)
        if not left:
            return total.reshape(self.share, -1)
        total = total.reshape((2,) * len(left) + (self.share, keep.shape[-1]))
        mask = self.masks[step + 1]
        place = left.index(mask)
        mine = self.bit(mask)
        send = pick(total, place, 1 - mine).astype(low)
        keep = pick(total, place, mine)
        return send.reshape(-1, send.shape[-1]), keep.reshape(-1, keep.shape[-1])

    def rest(self, step, keep, received):
        while step + 1 < len(self.masks):
            send, keep = self.join(step, keep, received)
            step += 1
            received = self.move(step, send)
        return self.join(step, keep, received)

    def move(self, step, send):
        return swap(send, "seq", self.masks[step])


class Vectors:
    def __init__(self, share):
        self.share = share
        self.count = lax.axis_size("seq")
        self.index = lax.axis_index("seq")

    def start(self, *vectors):
        total = jnp.concatenate(vectors, axis=0)
        return total.reshape(total.shape[0], self.count, self.share).transpose(1, 0, 2)

    def halve(self, kept, received):
        total = kept + received
        half = total.shape[0] // 2
        mine = (self.index // half) % 2
        view = total.reshape((2, half) + total.shape[1:])
        return pick(view, 0, 1 - mine), pick(view, 0, mine)

    def move(self, sent):
        return swap(sent, "seq", sent.shape[0])

    def end(self, kept, received):
        while kept.shape[0] > 1:
            sent, kept = self.halve(kept, received)
            received = self.move(sent)
        return (kept + received)[0]


def sum_over_x(block):
    count = lax.axis_size("tp")
    total = block
    mask = 2
    while mask < count:
        total = total.astype(low)
        total = total.astype(wide) + swap(total, "tp", mask).astype(wide)
        mask *= 2
    return total


def body(
    tokens,
    lengths,
    norm1_gain,
    in_weight,
    conv_weight,
    out_weight,
    norm2_gain,
    gate_weight,
    up_weight,
    down_weight,
    cotangent,
):
    micro_count, seq_count, shard_length, width = tokens.shape
    tp_count, tp_index = lax.axis_size("tp"), lax.axis_index("tp")
    seq_total, seq_index = lax.axis_size("seq"), lax.axis_index("seq")
    core = tp_index % 2
    own_micro = micro_count // 2
    rows = own_micro * seq_count * shard_length
    groups = own_micro * seq_count
    in_share = in_weight.shape[1] // tp_count
    out_share = width // tp_count
    share = width // seq_total
    masks = []
    mask = 1
    while mask < seq_total:
        masks.append(mask)
        mask *= 2
    spread = Spread(masks, share)
    taps = conv_weight.astype(wide)
    positions = seq_index * shard_length + jnp.arange(shard_length, dtype=jnp.int32)

    def micro_half(array, which):
        return lax.dynamic_slice_in_dim(array, which * own_micro, own_micro, 0)

    def row_mask(which):
        half = micro_half(lengths, which)
        return (positions[None, None, :] < half[:, :, None]).astype(wide).reshape(rows, 1)

    order = Order()
    none = jnp.int32(0)
    hidden = gate_weight.shape[1]

    def both_cores(own, other):
        own = own.reshape(own_micro, seq_count, shard_length, width)
        other = other.reshape(own_micro, seq_count, shard_length, width)
        return jnp.where(
            core == 0,
            jnp.concatenate([own, other], axis=0),
            jnp.concatenate([other, own], axis=0),
        )

    inputs = micro_half(tokens, core).astype(wide).reshape(rows, width)
    scale_one = lax.rsqrt(jnp.mean(inputs * inputs, axis=-1, keepdims=True) + eps)
    normed_one_f = inputs * scale_one
    normed_one = (normed_one_f * norm1_gain).astype(low)
    b_part = matmul(normed_one, in_weight[:, :width])
    x_part = matmul(normed_one, in_weight[:, 2 * width :])
    product = (b_part * x_part).astype(low).reshape(groups, shard_length, width)
    before = shift_blocks(product[:, shard_length - 2 :], 1)
    c_part = matmul(normed_one, in_weight[:, width : 2 * width])
    extended = jnp.concatenate([before, product], axis=1).astype(wide)
    conv_out = (
        taps[0] * extended[:, 0:shard_length]
        + taps[1] * extended[:, 1 : shard_length + 1]
        + taps[2] * extended[:, 2 : shard_length + 2]
    ).reshape(rows, width)
    gated_out = (c_part * conv_out).astype(low)
    residual = inputs + matmul(gated_out, out_weight)
    scale_two = lax.rsqrt(jnp.mean(residual * residual, axis=-1, keepdims=True) + eps)
    normed_two_f = residual * scale_two
    normed_own = (normed_two_f * norm2_gain).astype(low)
    normed_other = swap(normed_own, "tp", 1)

    own_mask = row_mask(core)
    out_grad = micro_half(cotangent, core).astype(wide).reshape(rows, width) * own_mask
    other_grad = micro_half(cotangent, 1 - core).astype(wide).reshape(rows, width) * row_mask(
        1 - core
    )
    low_own, low_other = out_grad.astype(low), other_grad.astype(low)

    def expand(normed):
        gate_proj = matmul(normed, gate_weight)
        up_proj = matmul(normed, up_weight)
        activated = (gate_proj * jax.nn.sigmoid(gate_proj) * up_proj).astype(low)
        return activated, gate_proj, up_proj

    def back(out_low, gate_proj, up_proj):
        sigmoid_gate = jax.nn.sigmoid(gate_proj)
        act_grad = matmul_nt(out_low, down_weight)
        gate_grad = (
            act_grad * up_proj * sigmoid_gate * (1.0 + gate_proj * (1.0 - sigmoid_gate))
        ).astype(low)
        return gate_grad, (act_grad * gate_proj * sigmoid_gate).astype(low)

    def two_terms(gate_grad, up_grad):
        return matmul_nt(gate_grad, gate_weight) + matmul_nt(up_grad, up_weight)

    def grad_part(kept):
        return lambda *pairs: spread.local([[pairs[:2], pairs[2:]]], [hidden], none, kept)

    def joined(step):
        return functools.partial(spread.join, step)

    act_own, gate_own, up_own = order(expand, normed_own)
    act_other, gate_other, up_other = order(expand, normed_other)
    down = (low_own, act_own, low_other, act_other)
    down_moved = spread.move(0, order(grad_part(False), *down))
    gate_grad_other, up_grad_other = order(back, low_other, gate_other, up_other)
    two_other = order(lambda *v: two_terms(*v).astype(low), gate_grad_other, up_grad_other)
    two_moved = swap(two_other, "tp", 1)
    ffn_other = order(lambda a: matmul(a, down_weight).astype(low), act_other)
    ffn_moved = swap(ffn_other, "tp", 1)
    gate_grad_own, up_grad_own = order(back, low_own, gate_own, up_own)
    two_own = order(two_terms, gate_grad_own, up_grad_own)
    ffn_own = order(lambda a: matmul(a, down_weight), act_own)
    two_half = order(lambda a, c: (a + c.astype(wide)).astype(low), two_own, two_moved)
    norm_two_grad = sum_over_x(two_half)
    gate = (normed_own, gate_grad_own, normed_other, gate_grad_other)
    up = (normed_own, up_grad_own, normed_other, up_grad_other)
    down_kept = order(grad_part(True), *down)
    gate_kept = order(grad_part(True), *gate)
    up_kept = order(grad_part(True), *up)
    gate_moved = spread.move(0, order(grad_part(False), *gate))
    down_sent, down_kept = order(joined(0), down_kept, down_moved)
    down_moved = spread.move(1, down_sent)
    ffn_half = order(lambda a, c: (a + c.astype(wide)).astype(low), ffn_own, ffn_moved)

    def to_residual(norm_two_grad, residual, scale_two, out_grad, c_part):
        normed_two_f = residual * scale_two
        grad_norm2 = jnp.sum(norm_two_grad * normed_two_f, axis=0)
        weighted_two = norm_two_grad * norm2_gain
        residual_grad = out_grad + scale_two * (
            weighted_two
            - normed_two_f * jnp.mean(weighted_two * normed_two_f, axis=-1, keepdims=True)
        )
        residual_low = residual_grad.astype(low)
        gated_grad = matmul_nt(residual_low, out_weight)
        conv_grad = (gated_grad * c_part).astype(low).reshape(groups, shard_length, width)
        return grad_norm2, residual_grad, residual_low, gated_grad, conv_grad

    grad_norm2, residual_grad, residual_low, gated_grad, conv_grad = order(
        to_residual, norm_two_grad, residual, scale_two, out_grad, c_part
    )
    after = shift_blocks(conv_grad[:, :2], -1)
    ffn_half, _ = lax.optimization_barrier((ffn_half, norm_two_grad))
    ffn_out = sum_over_x(ffn_half)
    down_sent, down_kept = order(joined(1), down_kept, down_moved)
    down_moved = spread.move(2, down_sent)

    def to_projected(conv_grad, after, extended, gated_grad, b_part, x_part, conv_out):
        ext_back = jnp.concatenate([conv_grad, after], axis=1).astype(wide)
        conv_grad_wide = ext_back[:, :shard_length]
        grad_conv = jnp.stack(
            [
                jnp.sum(conv_grad_wide * extended[:, offset : offset + shard_length], axis=(0, 1))
                for offset in range(taps.shape[0])
            ]
        )
        product_grad = (
            taps[0] * ext_back[:, 2 : shard_length + 2]
            + taps[1] * ext_back[:, 1 : shard_length + 1]
            + taps[2] * ext_back[:, 0:shard_length]
        ).reshape(rows, width)
        projected_grad = jnp.concatenate(
            [product_grad * x_part, gated_grad * conv_out, product_grad * b_part], axis=-1
        ).astype(low)
        return grad_conv, projected_grad

    grad_conv, projected_grad = order(
        to_projected, conv_grad, after, extended, gated_grad, b_part, x_part, conv_out
    )
    shares = [in_share, out_share]
    peer = tp_index + 1 - 2 * core

    def tail_part(columns, kept):
        def part(a, b, c, d, add=None):
            return spread.local([[(a, b)], [(c, d)]], shares, columns, kept, add)

        return part

    tail = (normed_one, projected_grad, gated_out, residual_low)
    tail_sent = swap(order(tail_part(peer, False), *tail), "tp", 1)
    tail_kept = swap(order(tail_part(peer, True), *tail), "tp", 1)

    def to_tokens(projected_grad, inputs, scale_one, residual_grad):
        normed_one_f = inputs * scale_one
        norm_one_grad = matmul_nt(projected_grad, in_weight)
        grad_norm1 = jnp.sum(norm_one_grad * normed_one_f, axis=0)
        weighted_one = norm_one_grad * norm1_gain
        input_grad = residual_grad + scale_one * (
            weighted_one
            - normed_one_f * jnp.mean(weighted_one * normed_one_f, axis=-1, keepdims=True)
        )
        return input_grad.astype(low), grad_norm1

    vectors = Vectors(share)
    gate_sent, gate_kept = order(joined(0), gate_kept, gate_moved)
    gate_moved = spread.move(1, gate_sent)
    up_moved = spread.move(0, order(grad_part(False), *up))
    input_grad, grad_norm1 = order(to_tokens, projected_grad, inputs, scale_one, residual_grad)
    input_moved = swap(input_grad, "tp", 1)
    vector_kept = order(vectors.start, grad_norm1[None], grad_norm2[None], grad_conv)
    vector_moved = swap(vector_kept, "tp", 1)
    tail_kept = order(tail_part(tp_index, True), *tail, tail_kept)
    grad_down = order(functools.partial(spread.rest, 2), down_kept, down_moved)
    grad_down = lax.optimization_barrier(grad_down).T
    vector_sent, vector_kept = order(vectors.halve, vector_kept, vector_moved)
    vector_moved = vectors.move(vector_sent)
    gate_sent, gate_kept = order(joined(1), gate_kept, gate_moved)
    gate_moved = spread.move(2, gate_sent)
    mixed_own = order(lambda r, f: ((r + f) * own_mask).astype(low), residual, ffn_out)
    mixed_moved = swap(mixed_own, "tp", 1)
    tokens_grad = order(both_cores, input_grad, input_moved)
    vector_sent, vector_kept = order(vectors.halve, vector_kept, vector_moved)
    vector_moved = vectors.move(vector_sent)
    tail_sent = order(tail_part(tp_index, False), *tail, tail_sent)
    up_sent, up_kept = order(joined(0), up_kept, up_moved)
    up_moved = spread.move(1, up_sent)
    tail_moved = spread.move(0, tail_sent)
    mixed = order(both_cores, mixed_own, mixed_moved)
    vector_sent, vector_kept = order(vectors.halve, vector_kept, vector_moved)
    vector_moved = vectors.move(vector_sent)
    grad_gate = order(functools.partial(spread.rest, 2), gate_kept, gate_moved)
    up_sent, up_kept = order(joined(1), up_kept, up_moved)
    up_moved = spread.move(2, up_sent)
    small = order(vectors.end, vector_kept, vector_moved)
    tail_sent, tail_kept = order(joined(0), tail_kept, tail_moved)
    tail_moved = spread.move(1, tail_sent)
    grad_up = order(functools.partial(spread.rest, 2), up_kept, up_moved)
    tail_sent, tail_kept = order(joined(1), tail_kept, tail_moved)
    tail_moved = spread.move(2, tail_sent)
    tail = order(functools.partial(spread.rest, 2), tail_kept, tail_moved)
    grad_in, grad_out = tail[:, :in_share], tail[:, in_share:]
    return (
        mixed,
        tokens_grad,
        small[0],
        grad_in,
        small[2:],
        grad_out,
        small[1],
        grad_gate,
        grad_up,
        grad_down,
    )


def solution(mesh):
    placed = (
        P(None, None, "seq", None),
        P(),
        P(),
        P(),
        P(),
        P(),
        P(),
        P(None, "tp"),
        P(None, "tp"),
        P("tp", None),
        P(None, None, "seq", None),
    )
    return jax.shard_map(
        body,
        mesh=mesh,
        in_specs=placed,
        out_specs=(
            P(None, None, "seq", None),
            P(None, None, "seq", None),
            P("seq"),
            P("seq", "tp"),
            P(None, "seq"),
            P("seq", "tp"),
            P("seq"),
            P("seq", "tp"),
            P("seq", "tp"),
            P("tp", "seq"),
        ),
        check_vma=False,
    )
```

```python
import functools

import jax
import jax.numpy as jnp
from jax import lax
from jax.experimental import pallas as pl
from jax.experimental.pallas import tpu as pltpu
from jax.sharding import PartitionSpec as P

eps = 1e-05
wide = jnp.float32
low = jnp.bfloat16


def tail_last_kernel(cuts, _, keep, received, grad_in, grad_out, small):
    total = keep[...].astype(wide) + received[...].astype(wide)
    grad_in[...] = total[:, : cuts[0]]
    grad_out[...] = total[:, cuts[0] : cuts[0] + cuts[1]]
    small[...] = total[:, cuts[0] + cuts[1] :].T[: small.shape[0]]


def tail_last(cuts, keep, received):
    rows = keep.shape[0]
    return kernel_call(
        functools.partial(tail_last_kernel, tuple(cuts)),
        [whole(keep), whole(received)],
        [((rows, c), wide, None, None) for c in cuts[:2]] + [((8, rows), wide, None, None)],
    )


def shift_blocks(block, distance):
    devices = range(lax.axis_size("seq"))
    route = [(i - distance, i) for i in devices if i - distance in devices]
    return lax.ppermute(block, "seq", route)


def swap(block, axis, mask):
    return lax.ppermute(block, axis, [(i, i ^ mask) for i in range(lax.axis_size(axis))])


def matmul(left, right):
    return jnp.dot(left, right, preferred_element_type=wide)


def matmul_nt(left, right):
    return lax.dot_general(left, right, (((1,), (1,)), ((), ())), preferred_element_type=wide)


def matmul_tn(left, right):
    return lax.dot_general(left, right, (((0,), (0,)), ((), ())), preferred_element_type=wide)


def pick(array, axis, index):
    return lax.dynamic_index_in_dim(array, index, axis, keepdims=False)


vmem_bytes = 20 * 2**20


def kernel_call(kernel, inputs, outputs, grid=(1,), scalars=None, scratch=(), room=vmem_bytes):
    scalars = jnp.zeros((1,), jnp.int32) if scalars is None else jnp.stack(scalars)

    def spec(shape, block, place):
        if block is None:
            zeros = (0,) * len(shape)
            return pl.BlockSpec(tuple(shape), lambda *_: zeros)
        return pl.BlockSpec(block, place)

    return pl.pallas_call(
        kernel,
        grid_spec=pltpu.PrefetchScalarGridSpec(
            num_scalar_prefetch=1,
            grid=grid,
            in_specs=[spec(a.shape, b, m) for a, b, m in inputs],
            out_specs=[spec(s, b, m) for s, _, b, m in outputs],
            scratch_shapes=list(scratch),
        ),
        out_shape=[jax.ShapeDtypeStruct(s, d) for s, d, _, _ in outputs],
        compiler_params=pltpu.CompilerParams(vmem_limit_bytes=room),
    )(scalars.astype(jnp.int32), *[a for a, _, _ in inputs])


def whole(array):
    return (array, None, None)


def normed(values, gain):
    scale = lax.rsqrt(jnp.mean(values * values, axis=-1, keepdims=True) + eps)
    return values * scale, scale


def front_kernel(_, tokens, gain, b_weight, x_weight, normed_one, product, b_part, x_part):
    @pl.when(pl.program_id(0) == 0)
    def _():
        inputs = tokens[...].astype(wide).reshape(normed_one.shape)
        scaled, _ = normed(inputs, None)
        normed_one[...] = (scaled * gain[...]).astype(low)

    b = matmul(normed_one[...], b_weight[...])
    x = matmul(normed_one[...], x_weight[...])
    product[...] = (b * x).astype(low)
    b_part[...] = b.astype(low)
    x_part[...] = x.astype(low)


def front(tokens, core, own_micro, gain, in_weight):
    _, seq_count, length, width = tokens.shape
    rows = own_micro * seq_count * length
    cut = width // 2
    column = ((rows, width), low, (rows, cut), lambda j, s: (0, j))
    return kernel_call(
        front_kernel,
        [
            (tokens, (own_micro, seq_count, length, width), lambda j, s: (s[0], 0, 0, 0)),
            whole(gain[None]),
            (in_weight, (width, cut), lambda j, s: (0, j)),
            (in_weight, (width, cut), lambda j, s: (0, 4 + j)),
        ],
        [((rows, width), low, None, None), column, column, column],
        grid=(2,),
        scalars=[core],
        room=60 * 2**20,
    )


def c_kernel(_, normed_one, weight, out):
    out[...] = matmul(normed_one[...], weight[...]).astype(low)


def c_columns(normed_one, in_weight):
    rows, width = normed_one.shape
    cut = width // 2
    return kernel_call(
        c_kernel,
        [whole(normed_one), (in_weight, (width, cut), lambda j, s: (0, 2 + j))],
        [((rows, width), low, (rows, cut), lambda j, s: (0, j))],
        grid=(2,),
        room=60 * 2**20,
    )[0]


def shifted_down(block, before, distance):
    moved = pltpu.roll(block, distance, 0)
    row = lax.broadcasted_iota(jnp.int32, block.shape, 0)
    for i in range(distance):
        moved = jnp.where(row == i, before[2 - distance + i : 3 - distance + i], moved)
    return moved


def middle_kernel(
    _, tokens, product, before, c_part, taps, out_weight, gain, gated, residual, normed_two
):
    step = pl.program_id(0)
    groups, length, _ = product.shape

    @pl.when(step == 0)
    def _():
        residual[...] = tokens[...].astype(wide).reshape(residual.shape)

    for g in range(groups):
        block = product[g].astype(wide)
        ahead = before[g].astype(wide)
        conv_out = (
            taps[0:1] * shifted_down(block, ahead, 2)
            + taps[1:2] * shifted_down(block, ahead, 1)
            + taps[2:3] * block
        )
        rows = slice(g * length, (g + 1) * length)
        gated[rows] = (c_part[rows].astype(wide) * conv_out).astype(low)
    residual[...] += matmul(gated[...], out_weight[...])

    @pl.when(step == pl.num_programs(0) - 1)
    def _():
        scaled, _ = normed(residual[...], None)
        normed_two[...] = (scaled * gain[...]).astype(low)


def middle(tokens, core, own_micro, product, before, c_part, taps, out_weight, gain):
    _, seq_count, length, width = tokens.shape
    groups = own_micro * seq_count
    rows = groups * length
    cut = width // 4
    return kernel_call(
        middle_kernel,
        [
            (tokens, (own_micro, seq_count, length, width), lambda k, s: (s[0], 0, 0, 0)),
            (product.reshape(groups, length, width), (groups, length, cut), lambda k, s: (0, 0, k)),
            (before, (groups, 2, cut), lambda k, s: (0, 0, k)),
            (c_part, (rows, cut), lambda k, s: (0, k)),
            (taps, (taps.shape[0], cut), lambda k, s: (0, k)),
            (out_weight, (cut, width), lambda k, s: (k, 0)),
            whole(gain[None]),
        ],
        [
            ((rows, width), low, (rows, cut), lambda k, s: (0, k)),
            ((rows, width), wide, None, None),
            ((rows, width), low, None, None),
        ],
        grid=(4,),
        scalars=[core],
    )


def assemble_kernel(_, own, other, out):
    @pl.when(pl.program_id(0) == 0)
    def _():
        out[...] = own[...].reshape(out.shape)

    @pl.when(pl.program_id(0) == 1)
    def _():
        out[...] = other[...].reshape(out.shape)


def assemble(own, other, core, own_micro, shape):
    block = (own_micro,) + tuple(shape[1:])
    return kernel_call(
        assemble_kernel,
        [whole(own), whole(other)],
        [(tuple(shape), low, block, lambda i, s: (jnp.where(i == 0, s[0], 1 - s[0]), 0, 0, 0))],
        grid=(2,),
        scalars=[core],
    )[0]


def mask_kernel(scalars, own, other, own_low, other_low, mask):
    micros, seqs, length, width = own.shape
    core, base = scalars[0], scalars[1]
    position = base + lax.broadcasted_iota(jnp.int32, (length, 1), 0)
    for source, which, out in ((own, core, own_low), (other, 1 - core, other_low)):
        for m in range(micros):
            for n in range(seqs):
                limit = scalars[2 + (which * micros + m) * seqs + n]
                keep = (position < limit).astype(wide)
                rows = slice((m * seqs + n) * length, (m * seqs + n + 1) * length)
                out[rows] = (source[m, n].astype(wide) * keep).astype(low)
                if out is own_low:
                    mask[rows] = keep


def masked(cotangent, lengths, core, base, own_micro):
    _, seq_count, length, width = cotangent.shape
    rows = own_micro * seq_count * length
    block = (own_micro, seq_count, length, width)
    return kernel_call(
        mask_kernel,
        [
            (cotangent, block, lambda i, s: (s[0], 0, 0, 0)),
            (cotangent, block, lambda i, s: (1 - s[0], 0, 0, 0)),
        ],
        [
            ((rows, width), low, None, None),
            ((rows, width), low, None, None),
            ((rows, 1), wide, None, None),
        ],
        scalars=[core, base, *lengths.reshape(-1)],
    )


def join_kernel(_, keep_send, got_send, keep_own, got_own, send, kept):
    send[...] = (
        (keep_send[...].astype(wide) + got_send[...].astype(wide)).reshape(send.shape).astype(low)
    )
    kept[...] = (
        (keep_own[...].astype(wide) + got_own[...].astype(wide)).reshape(kept.shape).astype(low)
    )


def join(keep, received, outer, bit):
    rows, columns = keep.shape
    inner = rows // (2 * outer)
    view = (outer, 2, inner, columns)
    block = (outer, 1, inner, columns)
    keep, received = keep.reshape(view), received.reshape(view)

    def send_place(i, s):
        return (0, 1 - s[0], 0, 0)

    def own_place(i, s):
        return (0, s[0], 0, 0)

    half = (rows // 2, columns)
    return kernel_call(
        join_kernel,
        [
            (keep, block, send_place),
            (received, block, send_place),
            (keep, block, own_place),
            (received, block, own_place),
        ],
        [(half, low, None, None), (half, low, None, None)],
        scalars=[bit],
    )


def last_kernel(cuts, turn, _, keep, received, *outs):
    total = keep[...].astype(wide) + received[...].astype(wide)
    start = 0
    for cut, out in zip(cuts, outs):
        part = total[:, start : start + cut]
        out[...] = part.T if turn else part
        start += cut


def join_last(keep, received, cuts, turn=False):
    rows = keep.shape[0]
    shapes = [(c, rows) if turn else (rows, c) for c in cuts]
    return kernel_call(
        functools.partial(last_kernel, tuple(cuts), turn),
        [whole(keep), whole(received)],
        [(s, wide, None, None) for s in shapes],
    )
sequence = (
    "expand own",
    "expand other",
    "send down",
    "back other",
    "two other",
    "ffn other",
    "back own",
    "two own",
    "ffn own",
    "two half",
    "keep down",
    "send gate",
    "join0 down",
    "ffn half",
    "keep gate",
    "residual",
    "send up",
    "join0 gate",
    "join1 down",
    "projected",
    "peer send",
    "peer keep",
    "tokens",
    "vector own",
    "keep up",
    "mixed half",
    "join0 up",
    "join1 gate",
    "end down",
    "vector sum",
    "send tail",
    "keep tail",
    "both tokens",
    "both mixed",
    "join1 up",
    "end gate",
    "join0 tail",
    "end up",
    "join1 tail",
    "tail end",
)


lanes = 128


def grad_kernel(blocks, pairs, has_add, select, *refs):
    del select
    out = refs[-1]
    add = refs[-2] if has_add else None
    start = 0
    refs = list(refs)
    for group in pairs:
        total = None
        for _ in range(group):
            lefts = [refs.pop(0)[...] for _ in range(blocks)]
            left = lefts[0] if blocks == 1 else jnp.concatenate(lefts, axis=1)
            term = matmul_tn(left, refs.pop(0)[...])
            total = term if total is None else total + term
        stop = start + total.shape[1]
        if has_add and stop <= add.shape[1]:
            total = total + add[:, start:stop].astype(wide)
        out[:, start:stop] = total.astype(out.dtype)
        start = stop


def weight_grad(groups, shares, columns, bit, mask, block, add=None):
    width = groups[0][0][0].shape[1]
    run = mask * block
    unit = run if run % lanes == 0 else width // 2
    count = width // 2 // unit
    select = jnp.stack([bit, *columns]).astype(jnp.int32)
    operands, specs = [], []

    def left_map(k):
        return lambda i, chosen: (0, 2 * k + chosen[0])

    def right_map(place):
        return lambda i, chosen: (0, chosen[1 + place])

    for place, (group, share) in enumerate(zip(groups, shares)):
        for left, right in group:
            rows = left.shape[0]
            if run % lanes:
                view = left.reshape(rows, width // (2 * run), 2, run)
                picked = lax.dynamic_index_in_dim(view, bit, 2, keepdims=False)
                operands.append(picked.reshape(rows, width // 2))
                specs.append(pl.BlockSpec((rows, width // 2), lambda i, chosen: (0, 0)))
            else:
                for k in range(count):
                    operands.append(left)
                    specs.append(pl.BlockSpec((rows, unit), left_map(k)))
            operands.append(right)
            specs.append(pl.BlockSpec((rows, share), right_map(place)))
    total = sum(shares)
    if add is not None:
        operands.append(add)
        specs.append(pl.BlockSpec(add.shape, lambda i, chosen: (0, 0)))
    return pl.pallas_call(
        functools.partial(grad_kernel, count, tuple(len(g) for g in groups), add is not None),
        grid_spec=pltpu.PrefetchScalarGridSpec(
            num_scalar_prefetch=1,
            grid=(1,),
            in_specs=specs,
            out_specs=pl.BlockSpec((width // 2, total), lambda i, chosen: (0, 0)),
        ),
        out_shape=jax.ShapeDtypeStruct((width // 2, total), low),
        compiler_params=pltpu.CompilerParams(vmem_limit_bytes=vmem_bytes),
    )(select, *operands)


def expand(normed, gate_weight, up_weight):
    gate = matmul(normed, gate_weight)
    up = matmul(normed, up_weight)
    sigmoid = jax.nn.sigmoid(gate)
    return (gate * sigmoid * up).astype(low), gate, up


def back(out_low, down_weight, gate, up):
    sigmoid = jax.nn.sigmoid(gate)
    act_grad = matmul_nt(out_low, down_weight)
    gate_grad = act_grad * up * sigmoid * (1.0 + gate * (1.0 - sigmoid))
    return gate_grad.astype(low), (act_grad * gate * sigmoid).astype(low)


def two_terms(gate_grad, up_grad, gate_weight, up_weight):
    return matmul_nt(gate_grad, gate_weight) + matmul_nt(up_grad, up_weight)


def conv_forward(product, before, taps):
    groups, length, width = product.shape
    extended = jnp.concatenate([before, product], axis=1).astype(wide)
    terms = [extended[:, k : k + length] for k in range(taps.shape[0])]
    return terms, sum(taps[k] * term for k, term in enumerate(terms))


def to_residual(first, second, residual, out_low, gain, out_weight, c_part):
    grad = first.astype(wide) + second.astype(wide)
    scaled, scale = normed(residual, None)
    grad_norm2 = jnp.sum(grad * scaled, axis=0, keepdims=True)
    weighted = grad * gain
    residual_grad = out_low.astype(wide) + scale * (
        weighted - scaled * jnp.mean(weighted * scaled, axis=-1, keepdims=True)
    )
    residual_low = residual_grad.astype(low)
    gated_grad = matmul_nt(residual_low, out_weight)
    conv_grad = (gated_grad * c_part.astype(wide)).astype(low)
    return residual_grad, residual_low, gated_grad, conv_grad, grad_norm2


def to_projected(conv_grad, after, gated_grad, product, before, b_part, x_part, taps):
    terms, conv_out = conv_forward(product, before, taps)
    groups, length, width = product.shape
    rows = groups * length
    count = taps.shape[0]
    ext_back = jnp.concatenate([conv_grad.reshape(product.shape), after], axis=1).astype(wide)
    grad_conv = jnp.stack([jnp.sum(ext_back[:, :length] * term, axis=(0, 1)) for term in terms])
    product_grad = sum(
        taps[k] * ext_back[:, count - 1 - k : count - 1 - k + length] for k in range(count)
    ).reshape(rows, width)
    projected_grad = jnp.concatenate(
        [
            product_grad * x_part.astype(wide),
            gated_grad * conv_out.reshape(rows, width),
            product_grad * b_part.astype(wide),
        ],
        axis=-1,
    ).astype(low)
    return projected_grad, grad_conv


def to_tokens(projected_grad, in_weight, inputs, residual_grad, gain):
    grad = matmul_nt(projected_grad, in_weight)
    scaled, scale = normed(inputs.astype(wide).reshape(grad.shape), None)
    grad_norm1 = jnp.sum(grad * scaled, axis=0, keepdims=True)
    weighted = grad * gain
    input_grad = residual_grad + scale * (
        weighted - scaled * jnp.mean(weighted * scaled, axis=-1, keepdims=True)
    )
    return input_grad.astype(low), grad_norm1


class Order:
    def __init__(self, tick):
        self.last = None
        self.tick = tick

    def __call__(self, task, *values):
        if self.last is not None:
            values, _ = lax.optimization_barrier((values, self.last))
        result = task(*values)
        self.last = result
        return result

    def space(self):
        self.tick = self(lambda tick: tick + 1.0, self.tick)


class Spread:
    def __init__(self, masks, share):
        self.masks = masks
        self.share = share
        self.index = lax.axis_index("seq")

    def bit(self, mask):
        return (self.index // mask) % 2

    def local(self, groups, shares, columns, kept, add=None):
        mask = self.masks[0]
        mine = self.bit(mask)
        bit = mine if kept else 1 - mine
        return weight_grad(groups, shares, columns, bit, mask, self.share, add)

    def join(self, step, keep, received):
        gone = self.masks[: step + 1]
        left = [m for m in sorted(self.masks, reverse=True) if m not in gone]
        mask = self.masks[step + 1]
        return join(keep, received, 2 ** left.index(mask), self.bit(mask))

    def until_last(self, step, keep, received):
        while step + 1 < len(self.masks):
            send, keep = self.join(step, keep, received)
            step += 1
            received = self.move(step, send)
        return keep, received

    def rest(self, step, cuts, turn, keep, received):
        keep, received = self.until_last(step, keep, received)
        return join_last(keep, received, cuts, turn)

    def move(self, step, send):
        return swap(send, "seq", self.masks[step])


def over_x(block):
    count = lax.axis_size("tp")
    mask = 2
    while 2 * mask < count:
        block = (block.astype(wide) + swap(block, "tp", mask).astype(wide)).astype(low)
        mask *= 2
    return block, swap(block, "tp", mask)


def body(
    tokens,
    lengths,
    norm1_gain,
    in_weight,
    conv_weight,
    out_weight,
    norm2_gain,
    gate_weight,
    up_weight,
    down_weight,
    cotangent,
):
    micro_count, seq_count, shard_length, width = tokens.shape
    tp_count, tp_index = lax.axis_size("tp"), lax.axis_index("tp")
    seq_total, seq_index = lax.axis_size("seq"), lax.axis_index("seq")
    core = tp_index % 2
    own_micro = micro_count // 2
    groups = own_micro * seq_count
    in_share = in_weight.shape[1] // tp_count
    out_share = width // tp_count
    share = width // seq_total
    hidden = gate_weight.shape[1]
    masks = []
    mask = 1
    while mask < seq_total:
        masks.append(mask)
        mask *= 2
    spread = Spread(masks, share)
    order = Order(lengths.astype(wide))
    none = jnp.int32(0)
    taps = conv_weight.astype(wide)

    normed_one, product, b_part, x_part = front(tokens, core, own_micro, norm1_gain, in_weight)
    edge = product.reshape(groups, shard_length, width)[:, shard_length - 2 :]
    before = shift_blocks(edge, 1)
    normed_one, edge = lax.optimization_barrier((normed_one, edge))
    low_own, low_other, own_mask = masked(
        cotangent, lengths, core, seq_index * shard_length, own_micro
    )
    c_part = c_columns(normed_one, in_weight)
    gated_out, residual, normed_own = middle(
        tokens, core, own_micro, product, before, c_part, taps, out_weight, norm2_gain
    )
    normed_other = swap(normed_own, "tp", 1)

    weights = (gate_weight, up_weight)
    shares = [in_share, out_share, lanes]
    peer = tp_index + 1 - 2 * core
    view = product.reshape(groups, shard_length, width)
    inputs = lax.dynamic_slice_in_dim(tokens, core * own_micro, own_micro, 0)
    at = {"normed_own": normed_own, "normed_other": normed_other}

    def run(task, *names):
        return order(task, *[at[name] for name in names])

    def expand_own():
        at["act_own"], at["gate_own"], at["up_own"] = run(
            lambda a: expand(a, *weights), "normed_own"
        )

    def expand_other():
        at["act_other"], at["gate_other"], at["up_other"] = run(
            lambda a: expand(a, *weights), "normed_other"
        )

    def back_own():
        at["gate_grad_own"], at["up_grad_own"] = run(
            lambda a, b: back(low_own, down_weight, a, b), "gate_own", "up_own"
        )

    def back_other():
        at["gate_grad_other"], at["up_grad_other"] = run(
            lambda a, b: back(low_other, down_weight, a, b), "gate_other", "up_other"
        )

    def two_other():
        two = run(lambda *v: two_terms(*v, *weights).astype(low), "gate_grad_other", "up_grad_other")
        at["two_moved"] = swap(two, "tp", 1)

    def two_own():
        at["two_own"] = run(lambda *v: two_terms(*v, *weights), "gate_grad_own", "up_grad_own")

    def two_half():
        half = run(lambda a, c: (a + c.astype(wide)).astype(low), "two_own", "two_moved")
        at["two_first"], at["two_second"] = over_x(half)

    def ffn_other():
        ffn = run(lambda a: matmul(a, down_weight).astype(low), "act_other")
        at["ffn_moved"] = swap(ffn, "tp", 1)

    def ffn_own():
        at["ffn_own"] = run(lambda a: matmul(a, down_weight), "act_own")

    def ffn_half():
        half = run(lambda a, c: (a + c.astype(wide)).astype(low), "ffn_own", "ffn_moved")
        at["ffn_first"], at["ffn_second"] = over_x(half)

    hidden_pairs = {
        "down": (low_own, "act_own", low_other, "act_other"),
        "gate": (normed_own, "gate_grad_own", normed_other, "gate_grad_other"),
        "up": (normed_own, "up_grad_own", normed_other, "up_grad_other"),
    }

    def hidden_grad(name, kept):
        own_left, own, other_left, other = hidden_pairs[name]

        def part(a, b):
            return spread.local([[(own_left, a), (other_left, b)]], [hidden], [none], kept)

        return run(part, own, other)

    def send(name):
        def task():
            at[name + "_moved0"] = spread.move(0, hidden_grad(name, False))

        return task

    def keep(name):
        def task():
            at[name + "_kept0"] = hidden_grad(name, True)

        return task

    def join_step(name, step, plan=spread):
        def task():
            sent, kept = run(
                functools.partial(plan.join, step), f"{name}_kept{step}", f"{name}_moved{step}"
            )
            at[f"{name}_kept{step + 1}"] = kept
            at[f"{name}_moved{step + 1}"] = plan.move(step + 1, sent)

        return task

    def finish(name, turn):
        def task():
            (at["grad_" + name],) = run(
                functools.partial(spread.rest, 2, [hidden], turn), name + "_kept2", name + "_moved2"
            )

        return task

    def residual_back():
        (
            at["residual_grad"],
            at["residual_low"],
            at["gated_grad"],
            at["conv_grad"],
            at["grad_norm2"],
        ) = run(
            lambda *v: to_residual(*v, residual, low_own, norm2_gain, out_weight, c_part),
            "two_first",
            "two_second",
        )
        edge = at["conv_grad"].reshape(groups, shard_length, width)[:, :2]
        at["after"] = shift_blocks(edge, -1)

    def projected_back():
        at["projected_grad"], at["grad_conv"] = run(
            lambda a, b, c: to_projected(a, b, c, view, before, b_part, x_part, taps),
            "conv_grad",
            "after",
            "gated_grad",
        )

    def peer_part(name, kept):
        def part(a, b):
            groups_of = [[(normed_one, a)], [(gated_out, b)]]
            return spread.local(groups_of, shares[:2], [peer] * 2, kept)

        def task():
            at[name] = swap(run(part, "projected_grad", "residual_low"), "tp", 1)

        return task

    def tail_part(kept):
        def part(a, b, c, add):
            groups_of = [[(normed_one, a)], [(gated_out, b)], [(c, jnp.eye(lanes, dtype=low))]]
            return spread.local(groups_of, shares, [tp_index, tp_index, none], kept, add)

        def task():
            names = ("projected_grad", "residual_low", "vectors")
            if kept:
                at["tail_kept0"] = run(part, *names, "keep_term")
            else:
                at["tail_moved0"] = spread.move(0, run(part, *names, "send_term"))

        return task

    def tokens_back():
        at["input_grad"], at["grad_norm1"] = run(
            lambda a, b: to_tokens(a, in_weight, inputs, b, norm1_gain),
            "projected_grad",
            "residual_grad",
        )
        at["input_moved"] = swap(at["input_grad"], "tp", 1)

    def vector_own():
        at["vector_own"] = run(
            lambda *v: jnp.concatenate(v, axis=0), "grad_norm1", "grad_norm2", "grad_conv"
        )
        at["vector_moved"] = swap(at["vector_own"], "tp", 1)

    def vector_sum():
        at["vectors"] = run(
            lambda a, b: jnp.pad(a + b, ((0, lanes - a.shape[0]), (0, 0))).astype(low),
            "vector_own",
            "vector_moved",
        )

    def mixed_half():
        at["mixed_own"] = run(
            lambda a, b: (
                (residual + (a.astype(wide) + b.astype(wide))) * own_mask
            ).astype(low),
            "ffn_first",
            "ffn_second",
        )
        at["mixed_moved"] = swap(at["mixed_own"], "tp", 1)

    def both(result, own, other):
        def task():
            at[result] = run(
                lambda a, b: assemble(a, b, core, own_micro, tokens.shape), own, other
            )

        return task

    def tail_end():
        at["grad_in"], at["grad_out"], at["small"] = run(
            lambda *v: tail_last(shares, *spread.until_last(2, *v)), "tail_kept2", "tail_moved2"
        )

    tasks = {
        "expand own": expand_own,
        "expand other": expand_other,
        "back own": back_own,
        "back other": back_other,
        "two other": two_other,
        "two own": two_own,
        "two half": two_half,
        "ffn other": ffn_other,
        "ffn own": ffn_own,
        "ffn half": ffn_half,
        "residual": residual_back,
        "projected": projected_back,
        "peer send": peer_part("send_term", False),
        "peer keep": peer_part("keep_term", True),
        "tokens": tokens_back,
        "vector own": vector_own,
        "vector sum": vector_sum,
        "mixed half": mixed_half,
        "both tokens": both("tokens_grad", "input_grad", "input_moved"),
        "both mixed": both("mixed", "mixed_own", "mixed_moved"),
        "send tail": tail_part(False),
        "keep tail": tail_part(True),
        "tail end": tail_end,
        "space": order.space,
    }
    for name in ("down", "gate", "up"):
        tasks["send " + name] = send(name)
        tasks["keep " + name] = keep(name)
        tasks["end " + name] = finish(name, name == "down")
    for name in ("down", "gate", "up", "tail"):
        tasks["join0 " + name] = join_step(name, 0)
        tasks["join1 " + name] = join_step(name, 1)
    for name in sequence:
        tasks[name]()
    small = at["small"]
    return (
        at["mixed"],
        at["tokens_grad"],
        small[0],
        at["grad_in"],
        small[2 : 2 + taps.shape[0]],
        at["grad_out"],
        small[1],
        at["grad_gate"],
        at["grad_up"],
        at["grad_down"],
    )


def solution(mesh):
    placed = (
        P(None, None, "seq", None),
        P(),
        P(),
        P(),
        P(),
        P(),
        P(),
        P(None, "tp"),
        P(None, "tp"),
        P("tp", None),
        P(None, None, "seq", None),
    )
    return jax.shard_map(
        body,
        mesh=mesh,
        in_specs=placed,
        out_specs=(
            P(None, None, "seq", None),
            P(None, None, "seq", None),
            P("seq"),
            P("seq", "tp"),
            P(None, "seq"),
            P("seq", "tp"),
            P("seq"),
            P("seq", "tp"),
            P("seq", "tp"),
            P("tp", "seq"),
        ),
        check_vma=False,
    )
```

```python
import functools

import jax
import jax.numpy as jnp
from jax import lax
from jax.experimental import pallas as pl
from jax.experimental.pallas import tpu as pltpu
from jax.sharding import PartitionSpec as P

eps = 1e-05
wide = jnp.float32
low = jnp.bfloat16


def shift_blocks(block, distance):
    devices = range(lax.axis_size("seq"))
    route = [(i - distance, i) for i in devices if i - distance in devices]
    return lax.ppermute(block, "seq", route)


def swap(block, axis, mask):
    return lax.ppermute(block, axis, [(i, i ^ mask) for i in range(lax.axis_size(axis))])


def matmul(left, right):
    return jnp.dot(left, right, preferred_element_type=wide)


def matmul_nt(left, right):
    return lax.dot_general(left, right, (((1,), (1,)), ((), ())), preferred_element_type=wide)


def matmul_tn(left, right):
    return lax.dot_general(left, right, (((0,), (0,)), ((), ())), preferred_element_type=wide)


def pick(array, axis, index):
    return lax.dynamic_index_in_dim(array, index, axis, keepdims=False)


vmem_bytes = 20 * 2**20


def kernel_call(kernel, inputs, outputs, grid=(1,), scalars=None, scratch=(), room=vmem_bytes):
    scalars = jnp.zeros((1,), jnp.int32) if scalars is None else jnp.stack(scalars)

    def spec(shape, block, place):
        if block is None:
            zeros = (0,) * len(shape)
            return pl.BlockSpec(tuple(shape), lambda *_: zeros)
        return pl.BlockSpec(block, place)

    return pl.pallas_call(
        kernel,
        grid_spec=pltpu.PrefetchScalarGridSpec(
            num_scalar_prefetch=1,
            grid=grid,
            in_specs=[spec(a.shape, b, m) for a, b, m in inputs],
            out_specs=[spec(s, b, m) for s, _, b, m in outputs],
            scratch_shapes=list(scratch),
        ),
        out_shape=[jax.ShapeDtypeStruct(s, d) for s, d, _, _ in outputs],
        compiler_params=pltpu.CompilerParams(vmem_limit_bytes=room),
    )(scalars.astype(jnp.int32), *[a for a, _, _ in inputs])


def whole(array):
    return (array, None, None)


def normed(values, gain):
    scale = lax.rsqrt(jnp.mean(values * values, axis=-1, keepdims=True) + eps)
    return values * scale, scale


def front_kernel(_, tokens, gain, b_weight, x_weight, normed_one, product, b_part, x_part):
    @pl.when(pl.program_id(0) == 0)
    def _():
        inputs = tokens[...].astype(wide).reshape(normed_one.shape)
        scaled, _ = normed(inputs, None)
        normed_one[...] = (scaled * gain[...]).astype(low)

    b = matmul(normed_one[...], b_weight[...])
    x = matmul(normed_one[...], x_weight[...])
    product[...] = (b * x).astype(low)
    b_part[...] = b.astype(low)
    x_part[...] = x.astype(low)


def front(tokens, core, own_micro, gain, in_weight):
    _, seq_count, length, width = tokens.shape
    rows = own_micro * seq_count * length
    cut = width // 2
    column = ((rows, width), low, (rows, cut), lambda j, s: (0, j))
    return kernel_call(
        front_kernel,
        [
            (tokens, (own_micro, seq_count, length, width), lambda j, s: (s[0], 0, 0, 0)),
            whole(gain[None]),
            (in_weight, (width, cut), lambda j, s: (0, j)),
            (in_weight, (width, cut), lambda j, s: (0, 4 + j)),
        ],
        [((rows, width), low, None, None), column, column, column],
        grid=(2,),
        scalars=[core],
        room=60 * 2**20,
    )


def c_kernel(_, normed_one, weight, out):
    out[...] = matmul(normed_one[...], weight[...]).astype(low)


def c_columns(normed_one, in_weight):
    rows, width = normed_one.shape
    cut = width // 2
    return kernel_call(
        c_kernel,
        [whole(normed_one), (in_weight, (width, cut), lambda j, s: (0, 2 + j))],
        [((rows, width), low, (rows, cut), lambda j, s: (0, j))],
        grid=(2,),
        room=60 * 2**20,
    )[0]


def shifted_down(block, before, distance):
    moved = pltpu.roll(block, distance, 0)
    row = lax.broadcasted_iota(jnp.int32, block.shape, 0)
    for i in range(distance):
        moved = jnp.where(row == i, before[2 - distance + i : 3 - distance + i], moved)
    return moved


def middle_kernel(
    _, tokens, product, before, c_part, taps, out_weight, gain, gated, residual, normed_two
):
    step = pl.program_id(0)
    groups, length, _ = product.shape

    @pl.when(step == 0)
    def _():
        residual[...] = tokens[...].astype(wide).reshape(residual.shape)

    for g in range(groups):
        block = product[g].astype(wide)
        ahead = before[g].astype(wide)
        conv_out = (
            taps[0:1] * shifted_down(block, ahead, 2)
            + taps[1:2] * shifted_down(block, ahead, 1)
            + taps[2:3] * block
        )
        rows = slice(g * length, (g + 1) * length)
        gated[rows] = (c_part[rows].astype(wide) * conv_out).astype(low)
    residual[...] += matmul(gated[...], out_weight[...])

    @pl.when(step == pl.num_programs(0) - 1)
    def _():
        scaled, _ = normed(residual[...], None)
        normed_two[...] = (scaled * gain[...]).astype(low)


def middle(tokens, core, own_micro, product, before, c_part, taps, out_weight, gain):
    _, seq_count, length, width = tokens.shape
    groups = own_micro * seq_count
    rows = groups * length
    cut = width // 4
    return kernel_call(
        middle_kernel,
        [
            (tokens, (own_micro, seq_count, length, width), lambda k, s: (s[0], 0, 0, 0)),
            (product.reshape(groups, length, width), (groups, length, cut), lambda k, s: (0, 0, k)),
            (before, (groups, 2, cut), lambda k, s: (0, 0, k)),
            (c_part, (rows, cut), lambda k, s: (0, k)),
            (taps, (taps.shape[0], cut), lambda k, s: (0, k)),
            (out_weight, (cut, width), lambda k, s: (k, 0)),
            whole(gain[None]),
        ],
        [
            ((rows, width), low, (rows, cut), lambda k, s: (0, k)),
            ((rows, width), wide, None, None),
            ((rows, width), low, None, None),
        ],
        grid=(4,),
        scalars=[core],
    )


def assemble_kernel(_, own, other, out):
    @pl.when(pl.program_id(0) == 0)
    def _():
        out[...] = own[...].reshape(out.shape)

    @pl.when(pl.program_id(0) == 1)
    def _():
        out[...] = other[...].reshape(out.shape)


def assemble(own, other, core, own_micro, shape):
    block = (own_micro,) + tuple(shape[1:])
    return kernel_call(
        assemble_kernel,
        [whole(own), whole(other)],
        [(tuple(shape), low, block, lambda i, s: (jnp.where(i == 0, s[0], 1 - s[0]), 0, 0, 0))],
        grid=(2,),
        scalars=[core],
    )[0]


def mask_kernel(scalars, own, other, own_low, other_low, mask):
    micros, seqs, length, width = own.shape
    core, base = scalars[0], scalars[1]
    position = base + lax.broadcasted_iota(jnp.int32, (length, 1), 0)
    for source, which, out in ((own, core, own_low), (other, 1 - core, other_low)):
        for m in range(micros):
            for n in range(seqs):
                limit = scalars[2 + (which * micros + m) * seqs + n]
                keep = (position < limit).astype(wide)
                rows = slice((m * seqs + n) * length, (m * seqs + n + 1) * length)
                out[rows] = (source[m, n].astype(wide) * keep).astype(low)
                if out is own_low:
                    mask[rows] = keep


def masked(cotangent, lengths, core, base, own_micro):
    _, seq_count, length, width = cotangent.shape
    rows = own_micro * seq_count * length
    block = (own_micro, seq_count, length, width)
    return kernel_call(
        mask_kernel,
        [
            (cotangent, block, lambda i, s: (s[0], 0, 0, 0)),
            (cotangent, block, lambda i, s: (1 - s[0], 0, 0, 0)),
        ],
        [
            ((rows, width), low, None, None),
            ((rows, width), low, None, None),
            ((rows, 1), wide, None, None),
        ],
        scalars=[core, base, *lengths.reshape(-1)],
    )


def join_kernel(_, keep_send, got_send, keep_own, got_own, send, kept):
    send[...] = (
        (keep_send[...].astype(wide) + got_send[...].astype(wide)).reshape(send.shape).astype(low)
    )
    kept[...] = (keep_own[...].astype(wide) + got_own[...].astype(wide)).reshape(kept.shape)


def join(keep, received, outer, bit):
    rows, columns = keep.shape
    inner = rows // (2 * outer)
    view = (outer, 2, inner, columns)
    block = (outer, 1, inner, columns)
    keep, received = keep.reshape(view), received.reshape(view)

    def send_place(i, s):
        return (0, 1 - s[0], 0, 0)

    def own_place(i, s):
        return (0, s[0], 0, 0)

    half = (rows // 2, columns)
    return kernel_call(
        join_kernel,
        [
            (keep, block, send_place),
            (received, block, send_place),
            (keep, block, own_place),
            (received, block, own_place),
        ],
        [(half, low, None, None), (half, wide, None, None)],
        scalars=[bit],
    )


def last_kernel(cuts, turn, _, keep, received, *outs):
    total = keep[...].astype(wide) + received[...].astype(wide)
    start = 0
    for cut, out in zip(cuts, outs):
        part = total[:, start : start + cut]
        out[...] = part.T if turn else part
        start += cut


def join_last(keep, received, cuts, turn=False):
    rows = keep.shape[0]
    shapes = [(c, rows) if turn else (rows, c) for c in cuts]
    return kernel_call(
        functools.partial(last_kernel, tuple(cuts), turn),
        [whole(keep), whole(received)],
        [(s, wide, None, None) for s in shapes],
    )
lanes = 128


def grad_kernel(blocks, pairs, has_add, select, *refs):
    del select
    out = refs[-1]
    add = refs[-2] if has_add else None
    start = 0
    refs = list(refs)
    for group in pairs:
        total = None
        for _ in range(group):
            lefts = [refs.pop(0)[...] for _ in range(blocks)]
            left = lefts[0] if blocks == 1 else jnp.concatenate(lefts, axis=1)
            term = matmul_tn(left, refs.pop(0)[...])
            total = term if total is None else total + term
        stop = start + total.shape[1]
        if has_add:
            total = total + add[:, start:stop].astype(wide)
        out[:, start:stop] = total.astype(out.dtype)
        start = stop


def weight_grad(groups, shares, columns, bit, mask, block, add=None):
    width = groups[0][0][0].shape[1]
    run = mask * block
    unit = run if run % lanes == 0 else width // 2
    count = width // 2 // unit
    select = jnp.stack([bit, columns]).astype(jnp.int32)
    operands, specs = [], []

    def left_map(k):
        return lambda i, chosen: (0, 2 * k + chosen[0])

    for group, share in zip(groups, shares):
        for left, right in group:
            rows = left.shape[0]
            if run % lanes:
                view = left.reshape(rows, width // (2 * run), 2, run)
                picked = lax.dynamic_index_in_dim(view, bit, 2, keepdims=False)
                operands.append(picked.reshape(rows, width // 2))
                specs.append(pl.BlockSpec((rows, width // 2), lambda i, chosen: (0, 0)))
            else:
                for k in range(count):
                    operands.append(left)
                    specs.append(pl.BlockSpec((rows, unit), left_map(k)))
            operands.append(right)
            specs.append(pl.BlockSpec((rows, share), lambda i, chosen: (0, chosen[1])))
    total = sum(shares)
    if add is not None:
        operands.append(add)
        specs.append(pl.BlockSpec((width // 2, total), lambda i, chosen: (0, 0)))
    return pl.pallas_call(
        functools.partial(grad_kernel, count, tuple(len(g) for g in groups), add is not None),
        grid_spec=pltpu.PrefetchScalarGridSpec(
            num_scalar_prefetch=1,
            grid=(1,),
            in_specs=specs,
            out_specs=pl.BlockSpec((width // 2, total), lambda i, chosen: (0, 0)),
        ),
        out_shape=jax.ShapeDtypeStruct((width // 2, total), low),
        compiler_params=pltpu.CompilerParams(vmem_limit_bytes=vmem_bytes),
    )(select, *operands)


def expand(normed, gate_weight, up_weight):
    gate = matmul(normed, gate_weight)
    up = matmul(normed, up_weight)
    sigmoid = jax.nn.sigmoid(gate)
    return (gate * sigmoid * up).astype(low), gate, up


def back(out_low, down_weight, gate, up):
    sigmoid = jax.nn.sigmoid(gate)
    act_grad = matmul_nt(out_low, down_weight)
    gate_grad = act_grad * up * sigmoid * (1.0 + gate * (1.0 - sigmoid))
    return gate_grad.astype(low), (act_grad * gate * sigmoid).astype(low)


def two_terms(gate_grad, up_grad, gate_weight, up_weight):
    return matmul_nt(gate_grad, gate_weight) + matmul_nt(up_grad, up_weight)


def conv_forward(product, before, taps):
    groups, length, width = product.shape
    extended = jnp.concatenate([before, product], axis=1).astype(wide)
    terms = [extended[:, k : k + length] for k in range(taps.shape[0])]
    return terms, sum(taps[k] * term for k, term in enumerate(terms))


def to_residual(first, second, residual, out_low, gain, out_weight, c_part):
    grad = first.astype(wide) + second.astype(wide)
    scaled, scale = normed(residual, None)
    grad_norm2 = jnp.sum(grad * scaled, axis=0, keepdims=True)
    weighted = grad * gain
    residual_grad = out_low.astype(wide) + scale * (
        weighted - scaled * jnp.mean(weighted * scaled, axis=-1, keepdims=True)
    )
    residual_low = residual_grad.astype(low)
    gated_grad = matmul_nt(residual_low, out_weight)
    conv_grad = (gated_grad * c_part.astype(wide)).astype(low)
    return residual_grad, residual_low, gated_grad, conv_grad, grad_norm2


def to_projected(conv_grad, after, gated_grad, product, before, b_part, x_part, taps):
    terms, conv_out = conv_forward(product, before, taps)
    groups, length, width = product.shape
    rows = groups * length
    count = taps.shape[0]
    ext_back = jnp.concatenate([conv_grad.reshape(product.shape), after], axis=1).astype(wide)
    grad_conv = jnp.stack([jnp.sum(ext_back[:, :length] * term, axis=(0, 1)) for term in terms])
    product_grad = sum(
        taps[k] * ext_back[:, count - 1 - k : count - 1 - k + length] for k in range(count)
    ).reshape(rows, width)
    projected_grad = jnp.concatenate(
        [
            product_grad * x_part.astype(wide),
            gated_grad * conv_out.reshape(rows, width),
            product_grad * b_part.astype(wide),
        ],
        axis=-1,
    ).astype(low)
    return projected_grad, grad_conv


def to_tokens(projected_grad, in_weight, inputs, residual_grad, gain):
    grad = matmul_nt(projected_grad, in_weight)
    scaled, scale = normed(inputs.astype(wide).reshape(grad.shape), None)
    grad_norm1 = jnp.sum(grad * scaled, axis=0, keepdims=True)
    weighted = grad * gain
    input_grad = residual_grad + scale * (
        weighted - scaled * jnp.mean(weighted * scaled, axis=-1, keepdims=True)
    )
    return input_grad.astype(low), grad_norm1


class Order:
    def __init__(self):
        self.last = None

    def __call__(self, task, *values):
        if self.last is not None:
            values, _ = lax.optimization_barrier((values, self.last))
        result = task(*values)
        self.last = result
        return result


class Spread:
    def __init__(self, masks, share):
        self.masks = masks
        self.share = share
        self.index = lax.axis_index("seq")

    def bit(self, mask):
        return (self.index // mask) % 2

    def local(self, groups, shares, columns, kept, add=None):
        mask = self.masks[0]
        mine = self.bit(mask)
        bit = mine if kept else 1 - mine
        return weight_grad(groups, shares, columns, bit, mask, self.share, add)

    def join(self, step, keep, received):
        gone = self.masks[: step + 1]
        left = [m for m in sorted(self.masks, reverse=True) if m not in gone]
        mask = self.masks[step + 1]
        return join(keep, received, 2 ** left.index(mask), self.bit(mask))

    def rest(self, step, cuts, turn, keep, received):
        while step + 1 < len(self.masks):
            send, keep = self.join(step, keep, received)
            step += 1
            received = self.move(step, send)
        return join_last(keep, received, cuts, turn)

    def move(self, step, send):
        return swap(send, "seq", self.masks[step])


class Vectors:
    def __init__(self, share):
        self.share = share
        self.count = lax.axis_size("seq")
        self.index = lax.axis_index("seq")

    def start(self, *vectors):
        total = jnp.concatenate(vectors, axis=0)
        return total.reshape(total.shape[0], self.count, self.share).transpose(1, 0, 2)

    def halve(self, kept, received):
        total = kept + received
        half = total.shape[0] // 2
        mine = (self.index // half) % 2
        view = total.reshape((2, half) + total.shape[1:])
        return pick(view, 0, 1 - mine), pick(view, 0, mine)

    def move(self, sent):
        return swap(sent, "seq", sent.shape[0])

    def end(self, kept, received):
        while kept.shape[0] > 1:
            sent, kept = self.halve(kept, received)
            received = self.move(sent)
        return (kept + received)[0]


def over_x(block):
    count = lax.axis_size("tp")
    mask = 2
    while 2 * mask < count:
        block = (block.astype(wide) + swap(block, "tp", mask).astype(wide)).astype(low)
        mask *= 2
    return block, swap(block, "tp", mask)


def body(
    tokens,
    lengths,
    norm1_gain,
    in_weight,
    conv_weight,
    out_weight,
    norm2_gain,
    gate_weight,
    up_weight,
    down_weight,
    cotangent,
):
    micro_count, seq_count, shard_length, width = tokens.shape
    tp_count, tp_index = lax.axis_size("tp"), lax.axis_index("tp")
    seq_total, seq_index = lax.axis_size("seq"), lax.axis_index("seq")
    core = tp_index % 2
    own_micro = micro_count // 2
    groups = own_micro * seq_count
    in_share = in_weight.shape[1] // tp_count
    out_share = width // tp_count
    share = width // seq_total
    hidden = gate_weight.shape[1]
    masks = []
    mask = 1
    while mask < seq_total:
        masks.append(mask)
        mask *= 2
    spread = Spread(masks, share)
    vectors = Vectors(share)
    order = Order()
    none = jnp.int32(0)
    taps = conv_weight.astype(wide)

    normed_one, product, b_part, x_part = front(tokens, core, own_micro, norm1_gain, in_weight)
    edge = product.reshape(groups, shard_length, width)[:, shard_length - 2 :]
    before = shift_blocks(edge, 1)
    normed_one, edge = lax.optimization_barrier((normed_one, edge))
    low_own, low_other, own_mask = masked(
        cotangent, lengths, core, seq_index * shard_length, own_micro
    )
    c_part = c_columns(normed_one, in_weight)
    gated_out, residual, normed_own = middle(
        tokens, core, own_micro, product, before, c_part, taps, out_weight, norm2_gain
    )
    normed_other = swap(normed_own, "tp", 1)

    def grad_part(kept):
        return lambda *pairs: spread.local([[pairs[:2], pairs[2:]]], [hidden], none, kept)

    def joined(step):
        return functools.partial(spread.join, step)

    def final(cuts, turn=False):
        return functools.partial(spread.rest, 2, cuts, turn)

    act_own, gate_own, up_own = order(expand, normed_own, gate_weight, up_weight)
    act_other, gate_other, up_other = order(expand, normed_other, gate_weight, up_weight)
    down = (low_own, act_own, low_other, act_other)
    down_moved = spread.move(0, order(grad_part(False), *down))
    gate_grad_other, up_grad_other = order(back, low_other, down_weight, gate_other, up_other)
    two_other = order(
        lambda *v: two_terms(*v, gate_weight, up_weight).astype(low), gate_grad_other, up_grad_other
    )
    two_moved = swap(two_other, "tp", 1)
    ffn_other = order(lambda a: matmul(a, down_weight).astype(low), act_other)
    ffn_moved = swap(ffn_other, "tp", 1)
    gate_grad_own, up_grad_own = order(back, low_own, down_weight, gate_own, up_own)
    two_own = order(lambda *v: two_terms(*v, gate_weight, up_weight), gate_grad_own, up_grad_own)
    ffn_own = order(lambda a: matmul(a, down_weight), act_own)
    two_half = order(lambda a, c: (a + c.astype(wide)).astype(low), two_own, two_moved)
    two_first, two_second = over_x(two_half)
    gate = (normed_own, gate_grad_own, normed_other, gate_grad_other)
    up = (normed_own, up_grad_own, normed_other, up_grad_other)
    down_kept = order(grad_part(True), *down)
    gate_moved = spread.move(0, order(grad_part(False), *gate))
    down_sent, down_kept = order(joined(0), down_kept, down_moved)
    down_moved = spread.move(1, down_sent)
    ffn_half = order(lambda a, c: (a + c.astype(wide)).astype(low), ffn_own, ffn_moved)
    gate_kept = order(grad_part(True), *gate)

    residual_grad, residual_low, gated_grad, conv_grad, grad_norm2 = order(
        lambda *v: to_residual(*v, norm2_gain, out_weight, c_part),
        two_first,
        two_second,
        residual,
        low_own,
    )
    after = shift_blocks(conv_grad.reshape(groups, shard_length, width)[:, :2], -1)
    ffn_half, _ = lax.optimization_barrier((ffn_half, two_second))
    ffn_first, ffn_second = over_x(ffn_half)
    up_moved = spread.move(0, order(grad_part(False), *up))
    gate_sent, gate_kept = order(joined(0), gate_kept, gate_moved)
    gate_moved = spread.move(1, gate_sent)
    down_sent, down_kept = order(joined(1), down_kept, down_moved)
    down_moved = spread.move(2, down_sent)
    view = product.reshape(groups, shard_length, width)
    projected_grad, grad_conv = order(
        lambda *v: to_projected(*v, taps),
        conv_grad,
        after,
        gated_grad,
        view,
        before,
        b_part,
        x_part,
    )
    shares = [in_share, out_share]
    peer = tp_index + 1 - 2 * core

    def tail_part(columns, kept):
        def part(a, b, c, d, add=None):
            return spread.local([[(a, b)], [(c, d)]], shares, columns, kept, add)

        return part

    tail = (normed_one, projected_grad, gated_out, residual_low)
    tail_sent = swap(order(tail_part(peer, False), *tail), "tp", 1)
    tail_kept = swap(order(tail_part(peer, True), *tail), "tp", 1)
    inputs = lax.dynamic_slice_in_dim(tokens, core * own_micro, own_micro, 0)
    input_grad, grad_norm1 = order(
        lambda a, b, c: to_tokens(a, in_weight, b, c, norm1_gain),
        projected_grad,
        inputs,
        residual_grad,
    )
    input_moved = swap(input_grad, "tp", 1)
    vector_kept = order(vectors.start, grad_norm1, grad_norm2, grad_conv)
    vector_moved = swap(vector_kept, "tp", 1)
    up_kept = order(grad_part(True), *up)
    mixed_own = order(
        lambda r, a, b: ((r + (a.astype(wide) + b.astype(wide))) * own_mask).astype(low),
        residual,
        ffn_first,
        ffn_second,
    )
    mixed_moved = swap(mixed_own, "tp", 1)
    up_sent, up_kept = order(joined(0), up_kept, up_moved)
    up_moved = spread.move(1, up_sent)
    gate_sent, gate_kept = order(joined(1), gate_kept, gate_moved)
    gate_moved = spread.move(2, gate_sent)
    (grad_down,) = order(final([hidden], True), down_kept, down_moved)
    vector_sent, vector_kept = order(vectors.halve, vector_kept, vector_moved)
    tail_sent = order(tail_part(tp_index, False), *tail, tail_sent)
    vector_moved = vectors.move(vector_sent)
    tail_moved = spread.move(0, tail_sent)
    tail_kept = order(tail_part(tp_index, True), *tail, tail_kept)

    def both(own, other):
        return assemble(own, other, core, own_micro, tokens.shape)

    tokens_grad = order(both, input_grad, input_moved)
    mixed = order(both, mixed_own, mixed_moved)
    up_sent, up_kept = order(joined(1), up_kept, up_moved)
    up_moved = spread.move(2, up_sent)
    (grad_gate,) = order(final([hidden]), gate_kept, gate_moved)
    tail_sent, tail_kept = order(joined(0), tail_kept, tail_moved)
    vector_sent, vector_kept = order(vectors.halve, vector_kept, vector_moved)
    vector_moved = vectors.move(vector_sent)
    tail_moved = spread.move(1, tail_sent)
    (grad_up,) = order(final([hidden]), up_kept, up_moved)
    tail_sent, tail_kept = order(joined(1), tail_kept, tail_moved)
    vector_sent, vector_kept = order(vectors.halve, vector_kept, vector_moved)
    vector_moved = vectors.move(vector_sent)
    tail_moved = spread.move(2, tail_sent)
    grad_in, grad_out = order(final(shares), tail_kept, tail_moved)
    small = order(vectors.end, vector_kept, vector_moved)
    return (
        mixed,
        tokens_grad,
        small[0],
        grad_in,
        small[2:],
        grad_out,
        small[1],
        grad_gate,
        grad_up,
        grad_down,
    )


def solution(mesh):
    placed = (
        P(None, None, "seq", None),
        P(),
        P(),
        P(),
        P(),
        P(),
        P(),
        P(None, "tp"),
        P(None, "tp"),
        P("tp", None),
        P(None, None, "seq", None),
    )
    return jax.shard_map(
        body,
        mesh=mesh,
        in_specs=placed,
        out_specs=(
            P(None, None, "seq", None),
            P(None, None, "seq", None),
            P("seq"),
            P("seq", "tp"),
            P(None, "seq"),
            P("seq", "tp"),
            P("seq"),
            P("seq", "tp"),
            P("seq", "tp"),
            P("tp", "seq"),
        ),
        check_vma=False,
    )
```

```python
import functools

import jax
import jax.numpy as jnp
from jax import lax
from jax.experimental import pallas as pl
from jax.experimental.pallas import tpu as pltpu
from jax.sharding import PartitionSpec as P

eps = 1e-05
wide = jnp.float32
low = jnp.bfloat16


def shift_blocks(block, distance):
    devices = range(lax.axis_size("seq"))
    route = [(i - distance, i) for i in devices if i - distance in devices]
    return lax.ppermute(block, "seq", route)


def swap(block, axis, mask):
    return lax.ppermute(block, axis, [(i, i ^ mask) for i in range(lax.axis_size(axis))])


def matmul(left, right):
    return jnp.dot(left, right, preferred_element_type=wide)


def matmul_nt(left, right):
    return lax.dot_general(left, right, (((1,), (1,)), ((), ())), preferred_element_type=wide)


def matmul_tn(left, right):
    return lax.dot_general(left, right, (((0,), (0,)), ((), ())), preferred_element_type=wide)


def pick(array, axis, index):
    return lax.dynamic_index_in_dim(array, index, axis, keepdims=False)


vmem_bytes = 20 * 2**20


def kernel_call(kernel, inputs, outputs, grid=(1,), scalars=None, scratch=(), room=vmem_bytes):
    scalars = jnp.zeros((1,), jnp.int32) if scalars is None else jnp.stack(scalars)

    def spec(shape, block, place):
        if block is None:
            zeros = (0,) * len(shape)
            return pl.BlockSpec(tuple(shape), lambda *_: zeros)
        return pl.BlockSpec(block, place)

    return pl.pallas_call(
        kernel,
        grid_spec=pltpu.PrefetchScalarGridSpec(
            num_scalar_prefetch=1,
            grid=grid,
            in_specs=[spec(a.shape, b, m) for a, b, m in inputs],
            out_specs=[spec(s, b, m) for s, _, b, m in outputs],
            scratch_shapes=list(scratch),
        ),
        out_shape=[jax.ShapeDtypeStruct(s, d) for s, d, _, _ in outputs],
        compiler_params=pltpu.CompilerParams(vmem_limit_bytes=room),
    )(scalars.astype(jnp.int32), *[a for a, _, _ in inputs])


def whole(array):
    return (array, None, None)


def normed(values, gain):
    scale = lax.rsqrt(jnp.mean(values * values, axis=-1, keepdims=True) + eps)
    return values * scale, scale


def front_kernel(_, tokens, gain, b_weight, x_weight, normed_one, product, b_part, x_part):
    @pl.when(pl.program_id(0) == 0)
    def _():
        inputs = tokens[...].astype(wide).reshape(normed_one.shape)
        scaled, _ = normed(inputs, None)
        normed_one[...] = (scaled * gain[...]).astype(low)

    b = matmul(normed_one[...], b_weight[...])
    x = matmul(normed_one[...], x_weight[...])
    product[...] = (b * x).astype(low)
    b_part[...] = b.astype(low)
    x_part[...] = x.astype(low)


def front(tokens, core, own_micro, gain, in_weight):
    _, seq_count, length, width = tokens.shape
    rows = own_micro * seq_count * length
    cut = width // 2
    column = ((rows, width), low, (rows, cut), lambda j, s: (0, j))
    return kernel_call(
        front_kernel,
        [
            (tokens, (own_micro, seq_count, length, width), lambda j, s: (s[0], 0, 0, 0)),
            whole(gain[None]),
            (in_weight, (width, cut), lambda j, s: (0, j)),
            (in_weight, (width, cut), lambda j, s: (0, 4 + j)),
        ],
        [((rows, width), low, None, None), column, column, column],
        grid=(2,),
        scalars=[core],
        room=60 * 2**20,
    )


def c_kernel(_, normed_one, weight, out):
    out[...] = matmul(normed_one[...], weight[...]).astype(low)


def c_columns(normed_one, in_weight):
    rows, width = normed_one.shape
    cut = width // 2
    return kernel_call(
        c_kernel,
        [whole(normed_one), (in_weight, (width, cut), lambda j, s: (0, 2 + j))],
        [((rows, width), low, (rows, cut), lambda j, s: (0, j))],
        grid=(2,),
        room=60 * 2**20,
    )[0]


def shifted_down(block, before, distance):
    moved = pltpu.roll(block, distance, 0)
    row = lax.broadcasted_iota(jnp.int32, block.shape, 0)
    for i in range(distance):
        moved = jnp.where(row == i, before[2 - distance + i : 3 - distance + i], moved)
    return moved


def middle_kernel(
    _, tokens, product, before, c_part, taps, out_weight, gain, gated, residual, normed_two
):
    step = pl.program_id(0)
    groups, length, _ = product.shape

    @pl.when(step == 0)
    def _():
        residual[...] = tokens[...].astype(wide).reshape(residual.shape)

    for g in range(groups):
        block = product[g].astype(wide)
        ahead = before[g].astype(wide)
        conv_out = (
            taps[0:1] * shifted_down(block, ahead, 2)
            + taps[1:2] * shifted_down(block, ahead, 1)
            + taps[2:3] * block
        )
        rows = slice(g * length, (g + 1) * length)
        gated[rows] = (c_part[rows].astype(wide) * conv_out).astype(low)
    residual[...] += matmul(gated[...], out_weight[...])

    @pl.when(step == pl.num_programs(0) - 1)
    def _():
        scaled, _ = normed(residual[...], None)
        normed_two[...] = (scaled * gain[...]).astype(low)


def middle(tokens, core, own_micro, product, before, c_part, taps, out_weight, gain):
    _, seq_count, length, width = tokens.shape
    groups = own_micro * seq_count
    rows = groups * length
    cut = width // 4
    return kernel_call(
        middle_kernel,
        [
            (tokens, (own_micro, seq_count, length, width), lambda k, s: (s[0], 0, 0, 0)),
            (product.reshape(groups, length, width), (groups, length, cut), lambda k, s: (0, 0, k)),
            (before, (groups, 2, cut), lambda k, s: (0, 0, k)),
            (c_part, (rows, cut), lambda k, s: (0, k)),
            (taps, (taps.shape[0], cut), lambda k, s: (0, k)),
            (out_weight, (cut, width), lambda k, s: (k, 0)),
            whole(gain[None]),
        ],
        [
            ((rows, width), low, (rows, cut), lambda k, s: (0, k)),
            ((rows, width), wide, None, None),
            ((rows, width), low, None, None),
        ],
        grid=(4,),
        scalars=[core],
    )


def assemble_kernel(_, own, other, out):
    @pl.when(pl.program_id(0) == 0)
    def _():
        out[...] = own[...].reshape(out.shape)

    @pl.when(pl.program_id(0) == 1)
    def _():
        out[...] = other[...].reshape(out.shape)


def assemble(own, other, core, own_micro, shape):
    block = (own_micro,) + tuple(shape[1:])
    return kernel_call(
        assemble_kernel,
        [whole(own), whole(other)],
        [(tuple(shape), low, block, lambda i, s: (jnp.where(i == 0, s[0], 1 - s[0]), 0, 0, 0))],
        grid=(2,),
        scalars=[core],
    )[0]


def mask_kernel(scalars, own, other, own_low, other_low, mask):
    micros, seqs, length, width = own.shape
    core, base = scalars[0], scalars[1]
    position = base + lax.broadcasted_iota(jnp.int32, (length, 1), 0)
    for source, which, out in ((own, core, own_low), (other, 1 - core, other_low)):
        for m in range(micros):
            for n in range(seqs):
                limit = scalars[2 + (which * micros + m) * seqs + n]
                keep = (position < limit).astype(wide)
                rows = slice((m * seqs + n) * length, (m * seqs + n + 1) * length)
                out[rows] = (source[m, n].astype(wide) * keep).astype(low)
                if out is own_low:
                    mask[rows] = keep


def masked(cotangent, lengths, core, base, own_micro):
    _, seq_count, length, width = cotangent.shape
    rows = own_micro * seq_count * length
    block = (own_micro, seq_count, length, width)
    return kernel_call(
        mask_kernel,
        [
            (cotangent, block, lambda i, s: (s[0], 0, 0, 0)),
            (cotangent, block, lambda i, s: (1 - s[0], 0, 0, 0)),
        ],
        [
            ((rows, width), low, None, None),
            ((rows, width), low, None, None),
            ((rows, 1), wide, None, None),
        ],
        scalars=[core, base, *lengths.reshape(-1)],
    )


def join_kernel(_, keep_send, got_send, keep_own, got_own, send, kept):
    send[...] = (
        (keep_send[...].astype(wide) + got_send[...].astype(wide)).reshape(send.shape).astype(low)
    )
    kept[...] = (
        (keep_own[...].astype(wide) + got_own[...].astype(wide)).reshape(kept.shape).astype(low)
    )


def join(keep, received, outer, bit):
    rows, columns = keep.shape
    inner = rows // (2 * outer)
    view = (outer, 2, inner, columns)
    block = (outer, 1, inner, columns)
    keep, received = keep.reshape(view), received.reshape(view)

    def send_place(i, s):
        return (0, 1 - s[0], 0, 0)

    def own_place(i, s):
        return (0, s[0], 0, 0)

    half = (rows // 2, columns)
    return kernel_call(
        join_kernel,
        [
            (keep, block, send_place),
            (received, block, send_place),
            (keep, block, own_place),
            (received, block, own_place),
        ],
        [(half, low, None, None), (half, low, None, None)],
        scalars=[bit],
    )


def last_kernel(cuts, turn, _, keep, received, *outs):
    total = keep[...].astype(wide) + received[...].astype(wide)
    start = 0
    for cut, out in zip(cuts, outs):
        part = total[:, start : start + cut]
        out[...] = part.T if turn else part
        start += cut


def join_last(keep, received, cuts, turn=False):
    rows = keep.shape[0]
    shapes = [(c, rows) if turn else (rows, c) for c in cuts]
    return kernel_call(
        functools.partial(last_kernel, tuple(cuts), turn),
        [whole(keep), whole(received)],
        [(s, wide, None, None) for s in shapes],
    )
lanes = 128


def grad_kernel(blocks, pairs, has_add, select, *refs):
    del select
    out = refs[-1]
    add = refs[-2] if has_add else None
    start = 0
    refs = list(refs)
    for group in pairs:
        total = None
        for _ in range(group):
            lefts = [refs.pop(0)[...] for _ in range(blocks)]
            left = lefts[0] if blocks == 1 else jnp.concatenate(lefts, axis=1)
            term = matmul_tn(left, refs.pop(0)[...])
            total = term if total is None else total + term
        stop = start + total.shape[1]
        if has_add:
            total = total + add[:, start:stop].astype(wide)
        out[:, start:stop] = total.astype(out.dtype)
        start = stop


def weight_grad(groups, shares, columns, bit, mask, block, add=None):
    width = groups[0][0][0].shape[1]
    run = mask * block
    unit = run if run % lanes == 0 else width // 2
    count = width // 2 // unit
    select = jnp.stack([bit, columns]).astype(jnp.int32)
    operands, specs = [], []

    def left_map(k):
        return lambda i, chosen: (0, 2 * k + chosen[0])

    for group, share in zip(groups, shares):
        for left, right in group:
            rows = left.shape[0]
            if run % lanes:
                view = left.reshape(rows, width // (2 * run), 2, run)
                picked = lax.dynamic_index_in_dim(view, bit, 2, keepdims=False)
                operands.append(picked.reshape(rows, width // 2))
                specs.append(pl.BlockSpec((rows, width // 2), lambda i, chosen: (0, 0)))
            else:
                for k in range(count):
                    operands.append(left)
                    specs.append(pl.BlockSpec((rows, unit), left_map(k)))
            operands.append(right)
            specs.append(pl.BlockSpec((rows, share), lambda i, chosen: (0, chosen[1])))
    total = sum(shares)
    if add is not None:
        operands.append(add)
        specs.append(pl.BlockSpec((width // 2, total), lambda i, chosen: (0, 0)))
    return pl.pallas_call(
        functools.partial(grad_kernel, count, tuple(len(g) for g in groups), add is not None),
        grid_spec=pltpu.PrefetchScalarGridSpec(
            num_scalar_prefetch=1,
            grid=(1,),
            in_specs=specs,
            out_specs=pl.BlockSpec((width // 2, total), lambda i, chosen: (0, 0)),
        ),
        out_shape=jax.ShapeDtypeStruct((width // 2, total), low),
        compiler_params=pltpu.CompilerParams(vmem_limit_bytes=vmem_bytes),
    )(select, *operands)


def expand(normed, gate_weight, up_weight):
    gate = matmul(normed, gate_weight)
    up = matmul(normed, up_weight)
    sigmoid = jax.nn.sigmoid(gate)
    return (gate * sigmoid * up).astype(low), gate, up


def back(out_low, down_weight, gate, up):
    sigmoid = jax.nn.sigmoid(gate)
    act_grad = matmul_nt(out_low, down_weight)
    gate_grad = act_grad * up * sigmoid * (1.0 + gate * (1.0 - sigmoid))
    return gate_grad.astype(low), (act_grad * gate * sigmoid).astype(low)


def two_terms(gate_grad, up_grad, gate_weight, up_weight):
    return matmul_nt(gate_grad, gate_weight) + matmul_nt(up_grad, up_weight)


def conv_forward(product, before, taps):
    groups, length, width = product.shape
    extended = jnp.concatenate([before, product], axis=1).astype(wide)
    terms = [extended[:, k : k + length] for k in range(taps.shape[0])]
    return terms, sum(taps[k] * term for k, term in enumerate(terms))


def to_residual(first, second, residual, out_low, gain, out_weight, c_part):
    grad = first.astype(wide) + second.astype(wide)
    scaled, scale = normed(residual, None)
    grad_norm2 = jnp.sum(grad * scaled, axis=0, keepdims=True)
    weighted = grad * gain
    residual_grad = out_low.astype(wide) + scale * (
        weighted - scaled * jnp.mean(weighted * scaled, axis=-1, keepdims=True)
    )
    residual_low = residual_grad.astype(low)
    gated_grad = matmul_nt(residual_low, out_weight)
    conv_grad = (gated_grad * c_part.astype(wide)).astype(low)
    return residual_grad, residual_low, gated_grad, conv_grad, grad_norm2


def to_projected(conv_grad, after, gated_grad, product, before, b_part, x_part, taps):
    terms, conv_out = conv_forward(product, before, taps)
    groups, length, width = product.shape
    rows = groups * length
    count = taps.shape[0]
    ext_back = jnp.concatenate([conv_grad.reshape(product.shape), after], axis=1).astype(wide)
    grad_conv = jnp.stack([jnp.sum(ext_back[:, :length] * term, axis=(0, 1)) for term in terms])
    product_grad = sum(
        taps[k] * ext_back[:, count - 1 - k : count - 1 - k + length] for k in range(count)
    ).reshape(rows, width)
    projected_grad = jnp.concatenate(
        [
            product_grad * x_part.astype(wide),
            gated_grad * conv_out.reshape(rows, width),
            product_grad * b_part.astype(wide),
        ],
        axis=-1,
    ).astype(low)
    return projected_grad, grad_conv


def to_tokens(projected_grad, in_weight, inputs, residual_grad, gain):
    grad = matmul_nt(projected_grad, in_weight)
    scaled, scale = normed(inputs.astype(wide).reshape(grad.shape), None)
    grad_norm1 = jnp.sum(grad * scaled, axis=0, keepdims=True)
    weighted = grad * gain
    input_grad = residual_grad + scale * (
        weighted - scaled * jnp.mean(weighted * scaled, axis=-1, keepdims=True)
    )
    return input_grad.astype(low), grad_norm1


class Order:
    def __init__(self):
        self.last = None

    def __call__(self, task, *values):
        if self.last is not None:
            values, _ = lax.optimization_barrier((values, self.last))
        result = task(*values)
        self.last = result
        return result


class Spread:
    def __init__(self, masks, share):
        self.masks = masks
        self.share = share
        self.index = lax.axis_index("seq")

    def bit(self, mask):
        return (self.index // mask) % 2

    def local(self, groups, shares, columns, kept, add=None):
        mask = self.masks[0]
        mine = self.bit(mask)
        bit = mine if kept else 1 - mine
        return weight_grad(groups, shares, columns, bit, mask, self.share, add)

    def join(self, step, keep, received):
        gone = self.masks[: step + 1]
        left = [m for m in sorted(self.masks, reverse=True) if m not in gone]
        mask = self.masks[step + 1]
        return join(keep, received, 2 ** left.index(mask), self.bit(mask))

    def rest(self, step, cuts, turn, keep, received):
        while step + 1 < len(self.masks):
            send, keep = self.join(step, keep, received)
            step += 1
            received = self.move(step, send)
        return join_last(keep, received, cuts, turn)

    def move(self, step, send):
        return swap(send, "seq", self.masks[step])


class Vectors:
    def __init__(self, share):
        self.share = share
        self.count = lax.axis_size("seq")
        self.index = lax.axis_index("seq")

    def start(self, *vectors):
        total = jnp.concatenate(vectors, axis=0)
        return total.reshape(total.shape[0], self.count, self.share).transpose(1, 0, 2)

    def halve(self, kept, received):
        total = kept + received
        half = total.shape[0] // 2
        mine = (self.index // half) % 2
        view = total.reshape((2, half) + total.shape[1:])
        return pick(view, 0, 1 - mine), pick(view, 0, mine)

    def move(self, sent):
        return swap(sent, "seq", sent.shape[0])

    def end(self, kept, received):
        while kept.shape[0] > 1:
            sent, kept = self.halve(kept, received)
            received = self.move(sent)
        return (kept + received)[0]


def over_x(block):
    count = lax.axis_size("tp")
    mask = 2
    while 2 * mask < count:
        block = (block.astype(wide) + swap(block, "tp", mask).astype(wide)).astype(low)
        mask *= 2
    return block, swap(block, "tp", mask)


def body(
    tokens,
    lengths,
    norm1_gain,
    in_weight,
    conv_weight,
    out_weight,
    norm2_gain,
    gate_weight,
    up_weight,
    down_weight,
    cotangent,
):
    micro_count, seq_count, shard_length, width = tokens.shape
    tp_count, tp_index = lax.axis_size("tp"), lax.axis_index("tp")
    seq_total, seq_index = lax.axis_size("seq"), lax.axis_index("seq")
    core = tp_index % 2
    own_micro = micro_count // 2
    groups = own_micro * seq_count
    in_share = in_weight.shape[1] // tp_count
    out_share = width // tp_count
    share = width // seq_total
    hidden = gate_weight.shape[1]
    masks = []
    mask = 1
    while mask < seq_total:
        masks.append(mask)
        mask *= 2
    spread = Spread(masks, share)
    vectors = Vectors(share)
    order = Order()
    none = jnp.int32(0)
    taps = conv_weight.astype(wide)

    normed_one, product, b_part, x_part = front(tokens, core, own_micro, norm1_gain, in_weight)
    edge = product.reshape(groups, shard_length, width)[:, shard_length - 2 :]
    before = shift_blocks(edge, 1)
    normed_one, edge = lax.optimization_barrier((normed_one, edge))
    low_own, low_other, own_mask = masked(
        cotangent, lengths, core, seq_index * shard_length, own_micro
    )
    c_part = c_columns(normed_one, in_weight)
    gated_out, residual, normed_own = middle(
        tokens, core, own_micro, product, before, c_part, taps, out_weight, norm2_gain
    )
    normed_other = swap(normed_own, "tp", 1)

    def grad_part(kept):
        return lambda *pairs: spread.local([[pairs[:2], pairs[2:]]], [hidden], none, kept)

    def joined(step):
        return functools.partial(spread.join, step)

    def final(cuts, turn=False):
        return functools.partial(spread.rest, 2, cuts, turn)

    act_own, gate_own, up_own = order(expand, normed_own, gate_weight, up_weight)
    act_other, gate_other, up_other = order(expand, normed_other, gate_weight, up_weight)
    down = (low_own, act_own, low_other, act_other)
    down_moved = spread.move(0, order(grad_part(False), *down))
    gate_grad_other, up_grad_other = order(back, low_other, down_weight, gate_other, up_other)
    two_other = order(
        lambda *v: two_terms(*v, gate_weight, up_weight).astype(low), gate_grad_other, up_grad_other
    )
    two_moved = swap(two_other, "tp", 1)
    ffn_other = order(lambda a: matmul(a, down_weight).astype(low), act_other)
    ffn_moved = swap(ffn_other, "tp", 1)
    gate_grad_own, up_grad_own = order(back, low_own, down_weight, gate_own, up_own)
    two_own = order(lambda *v: two_terms(*v, gate_weight, up_weight), gate_grad_own, up_grad_own)
    ffn_own = order(lambda a: matmul(a, down_weight), act_own)
    two_half = order(lambda a, c: (a + c.astype(wide)).astype(low), two_own, two_moved)
    two_first, two_second = over_x(two_half)
    gate = (normed_own, gate_grad_own, normed_other, gate_grad_other)
    up = (normed_own, up_grad_own, normed_other, up_grad_other)
    down_kept = order(grad_part(True), *down)
    gate_moved = spread.move(0, order(grad_part(False), *gate))
    down_sent, down_kept = order(joined(0), down_kept, down_moved)
    down_moved = spread.move(1, down_sent)
    ffn_half = order(lambda a, c: (a + c.astype(wide)).astype(low), ffn_own, ffn_moved)
    gate_kept = order(grad_part(True), *gate)

    up_moved = spread.move(0, order(grad_part(False), *up))

    residual_grad, residual_low, gated_grad, conv_grad, grad_norm2 = order(
        lambda *v: to_residual(*v, norm2_gain, out_weight, c_part),
        two_first,
        two_second,
        residual,
        low_own,
    )
    after = shift_blocks(conv_grad.reshape(groups, shard_length, width)[:, :2], -1)
    ffn_half, _ = lax.optimization_barrier((ffn_half, two_second))
    ffn_first, ffn_second = over_x(ffn_half)
    gate_sent, gate_kept = order(joined(0), gate_kept, gate_moved)
    gate_moved = spread.move(1, gate_sent)
    down_sent, down_kept = order(joined(1), down_kept, down_moved)
    down_moved = spread.move(2, down_sent)
    view = product.reshape(groups, shard_length, width)
    projected_grad, grad_conv = order(
        lambda *v: to_projected(*v, taps),
        conv_grad,
        after,
        gated_grad,
        view,
        before,
        b_part,
        x_part,
    )
    shares = [in_share, out_share]
    peer = tp_index + 1 - 2 * core

    def tail_part(columns, kept):
        def part(a, b, c, d, add=None):
            return spread.local([[(a, b)], [(c, d)]], shares, columns, kept, add)

        return part

    tail = (normed_one, projected_grad, gated_out, residual_low)
    tail_sent = swap(order(tail_part(peer, False), *tail), "tp", 1)
    tail_kept = swap(order(tail_part(peer, True), *tail), "tp", 1)
    inputs = lax.dynamic_slice_in_dim(tokens, core * own_micro, own_micro, 0)
    input_grad, grad_norm1 = order(
        lambda a, b, c: to_tokens(a, in_weight, b, c, norm1_gain),
        projected_grad,
        inputs,
        residual_grad,
    )
    input_moved = swap(input_grad, "tp", 1)
    gate_sent, gate_kept = order(joined(1), gate_kept, gate_moved)
    gate_moved = spread.move(2, gate_sent)
    vector_kept = order(vectors.start, grad_norm1, grad_norm2, grad_conv)
    vector_moved = swap(vector_kept, "tp", 1)
    up_kept = order(grad_part(True), *up)
    mixed_own = order(
        lambda r, a, b: ((r + (a.astype(wide) + b.astype(wide))) * own_mask).astype(low),
        residual,
        ffn_first,
        ffn_second,
    )
    mixed_moved = swap(mixed_own, "tp", 1)
    up_sent, up_kept = order(joined(0), up_kept, up_moved)
    up_moved = spread.move(1, up_sent)
    (grad_down,) = order(final([hidden], True), down_kept, down_moved)
    vector_sent, vector_kept = order(vectors.halve, vector_kept, vector_moved)
    tail_sent = order(tail_part(tp_index, False), *tail, tail_sent)
    vector_moved = vectors.move(vector_sent)
    tail_moved = spread.move(0, tail_sent)
    tail_kept = order(tail_part(tp_index, True), *tail, tail_kept)

    def both(own, other):
        return assemble(own, other, core, own_micro, tokens.shape)

    tokens_grad = order(both, input_grad, input_moved)
    mixed = order(both, mixed_own, mixed_moved)
    up_sent, up_kept = order(joined(1), up_kept, up_moved)
    up_moved = spread.move(2, up_sent)
    (grad_gate,) = order(final([hidden]), gate_kept, gate_moved)
    tail_sent, tail_kept = order(joined(0), tail_kept, tail_moved)
    vector_sent, vector_kept = order(vectors.halve, vector_kept, vector_moved)
    vector_moved = vectors.move(vector_sent)
    tail_moved = spread.move(1, tail_sent)
    (grad_up,) = order(final([hidden]), up_kept, up_moved)
    tail_sent, tail_kept = order(joined(1), tail_kept, tail_moved)
    vector_sent, vector_kept = order(vectors.halve, vector_kept, vector_moved)
    vector_moved = vectors.move(vector_sent)
    tail_moved = spread.move(2, tail_sent)
    grad_in, grad_out = order(final(shares), tail_kept, tail_moved)
    small = order(vectors.end, vector_kept, vector_moved)
    return (
        mixed,
        tokens_grad,
        small[0],
        grad_in,
        small[2:],
        grad_out,
        small[1],
        grad_gate,
        grad_up,
        grad_down,
    )


def solution(mesh):
    placed = (
        P(None, None, "seq", None),
        P(),
        P(),
        P(),
        P(),
        P(),
        P(),
        P(None, "tp"),
        P(None, "tp"),
        P("tp", None),
        P(None, None, "seq", None),
    )
    return jax.shard_map(
        body,
        mesh=mesh,
        in_specs=placed,
        out_specs=(
            P(None, None, "seq", None),
            P(None, None, "seq", None),
            P("seq"),
            P("seq", "tp"),
            P(None, "seq"),
            P("seq", "tp"),
            P("seq"),
            P("seq", "tp"),
            P("seq", "tp"),
            P("tp", "seq"),
        ),
        check_vma=False,
    )
```

```python
import functools

import jax
import jax.numpy as jnp
from jax import lax
from jax.experimental import pallas as pl
from jax.experimental.pallas import tpu as pltpu
from jax.sharding import PartitionSpec as P

eps = 1e-05
wide = jnp.float32
low = jnp.bfloat16


def shift_blocks(block, distance):
    devices = range(lax.axis_size("seq"))
    route = [(i - distance, i) for i in devices if i - distance in devices]
    return lax.ppermute(block, "seq", route)


def swap(block, axis, mask):
    return lax.ppermute(block, axis, [(i, i ^ mask) for i in range(lax.axis_size(axis))])


def matmul(left, right):
    return jnp.dot(left, right, preferred_element_type=wide)


def matmul_nt(left, right):
    return lax.dot_general(left, right, (((1,), (1,)), ((), ())), preferred_element_type=wide)


def matmul_tn(left, right):
    return lax.dot_general(left, right, (((0,), (0,)), ((), ())), preferred_element_type=wide)


def pick(array, axis, index):
    return lax.dynamic_index_in_dim(array, index, axis, keepdims=False)


vmem_bytes = 20 * 2**20


def kernel_call(kernel, inputs, outputs, grid=(1,), scalars=None, scratch=(), room=vmem_bytes):
    scalars = jnp.zeros((1,), jnp.int32) if scalars is None else jnp.stack(scalars)

    def spec(shape, block, place):
        if block is None:
            zeros = (0,) * len(shape)
            return pl.BlockSpec(tuple(shape), lambda *_: zeros)
        return pl.BlockSpec(block, place)

    return pl.pallas_call(
        kernel,
        grid_spec=pltpu.PrefetchScalarGridSpec(
            num_scalar_prefetch=1,
            grid=grid,
            in_specs=[spec(a.shape, b, m) for a, b, m in inputs],
            out_specs=[spec(s, b, m) for s, _, b, m in outputs],
            scratch_shapes=list(scratch),
        ),
        out_shape=[jax.ShapeDtypeStruct(s, d) for s, d, _, _ in outputs],
        compiler_params=pltpu.CompilerParams(vmem_limit_bytes=room),
    )(scalars.astype(jnp.int32), *[a for a, _, _ in inputs])


def whole(array):
    return (array, None, None)


def normed(values, gain):
    scale = lax.rsqrt(jnp.mean(values * values, axis=-1, keepdims=True) + eps)
    return values * scale, scale


def front_kernel(_, tokens, gain, b_weight, x_weight, normed_one, product, b_part, x_part):
    @pl.when(pl.program_id(0) == 0)
    def _():
        inputs = tokens[...].astype(wide).reshape(normed_one.shape)
        scaled, _ = normed(inputs, None)
        normed_one[...] = (scaled * gain[...]).astype(low)

    b = matmul(normed_one[...], b_weight[...])
    x = matmul(normed_one[...], x_weight[...])
    product[...] = (b * x).astype(low)
    b_part[...] = b.astype(low)
    x_part[...] = x.astype(low)


def front(tokens, core, own_micro, gain, in_weight):
    _, seq_count, length, width = tokens.shape
    rows = own_micro * seq_count * length
    cut = width // 2
    column = ((rows, width), low, (rows, cut), lambda j, s: (0, j))
    return kernel_call(
        front_kernel,
        [
            (tokens, (own_micro, seq_count, length, width), lambda j, s: (s[0], 0, 0, 0)),
            whole(gain[None]),
            (in_weight, (width, cut), lambda j, s: (0, j)),
            (in_weight, (width, cut), lambda j, s: (0, 4 + j)),
        ],
        [((rows, width), low, None, None), column, column, column],
        grid=(2,),
        scalars=[core],
        room=60 * 2**20,
    )


def c_kernel(_, normed_one, weight, out):
    out[...] = matmul(normed_one[...], weight[...]).astype(low)


def c_columns(normed_one, in_weight):
    rows, width = normed_one.shape
    cut = width // 2
    return kernel_call(
        c_kernel,
        [whole(normed_one), (in_weight, (width, cut), lambda j, s: (0, 2 + j))],
        [((rows, width), low, (rows, cut), lambda j, s: (0, j))],
        grid=(2,),
        room=60 * 2**20,
    )[0]


def shifted_down(block, before, distance):
    moved = pltpu.roll(block, distance, 0)
    row = lax.broadcasted_iota(jnp.int32, block.shape, 0)
    for i in range(distance):
        moved = jnp.where(row == i, before[2 - distance + i : 3 - distance + i], moved)
    return moved


def middle_kernel(
    _, tokens, product, before, c_part, taps, out_weight, gain, gated, residual, normed_two
):
    step = pl.program_id(0)
    groups, length, _ = product.shape

    @pl.when(step == 0)
    def _():
        residual[...] = tokens[...].astype(wide).reshape(residual.shape)

    for g in range(groups):
        block = product[g].astype(wide)
        ahead = before[g].astype(wide)
        conv_out = (
            taps[0:1] * shifted_down(block, ahead, 2)
            + taps[1:2] * shifted_down(block, ahead, 1)
            + taps[2:3] * block
        )
        rows = slice(g * length, (g + 1) * length)
        gated[rows] = (c_part[rows].astype(wide) * conv_out).astype(low)
    residual[...] += matmul(gated[...], out_weight[...])

    @pl.when(step == pl.num_programs(0) - 1)
    def _():
        scaled, _ = normed(residual[...], None)
        normed_two[...] = (scaled * gain[...]).astype(low)


def middle(tokens, core, own_micro, product, before, c_part, taps, out_weight, gain):
    _, seq_count, length, width = tokens.shape
    groups = own_micro * seq_count
    rows = groups * length
    cut = width // 4
    return kernel_call(
        middle_kernel,
        [
            (tokens, (own_micro, seq_count, length, width), lambda k, s: (s[0], 0, 0, 0)),
            (product.reshape(groups, length, width), (groups, length, cut), lambda k, s: (0, 0, k)),
            (before, (groups, 2, cut), lambda k, s: (0, 0, k)),
            (c_part, (rows, cut), lambda k, s: (0, k)),
            (taps, (taps.shape[0], cut), lambda k, s: (0, k)),
            (out_weight, (cut, width), lambda k, s: (k, 0)),
            whole(gain[None]),
        ],
        [
            ((rows, width), low, (rows, cut), lambda k, s: (0, k)),
            ((rows, width), wide, None, None),
            ((rows, width), low, None, None),
        ],
        grid=(4,),
        scalars=[core],
    )


def assemble_kernel(_, own, other, out):
    @pl.when(pl.program_id(0) == 0)
    def _():
        out[...] = own[...].reshape(out.shape)

    @pl.when(pl.program_id(0) == 1)
    def _():
        out[...] = other[...].reshape(out.shape)


def assemble(own, other, core, own_micro, shape):
    block = (own_micro,) + tuple(shape[1:])
    return kernel_call(
        assemble_kernel,
        [whole(own), whole(other)],
        [(tuple(shape), low, block, lambda i, s: (jnp.where(i == 0, s[0], 1 - s[0]), 0, 0, 0))],
        grid=(2,),
        scalars=[core],
    )[0]


def mask_kernel(scalars, own, other, own_low, other_low, mask):
    micros, seqs, length, width = own.shape
    core, base = scalars[0], scalars[1]
    position = base + lax.broadcasted_iota(jnp.int32, (length, 1), 0)
    for source, which, out in ((own, core, own_low), (other, 1 - core, other_low)):
        for m in range(micros):
            for n in range(seqs):
                limit = scalars[2 + (which * micros + m) * seqs + n]
                keep = (position < limit).astype(wide)
                rows = slice((m * seqs + n) * length, (m * seqs + n + 1) * length)
                out[rows] = (source[m, n].astype(wide) * keep).astype(low)
                if out is own_low:
                    mask[rows] = keep


def masked(cotangent, lengths, core, base, own_micro):
    _, seq_count, length, width = cotangent.shape
    rows = own_micro * seq_count * length
    block = (own_micro, seq_count, length, width)
    return kernel_call(
        mask_kernel,
        [
            (cotangent, block, lambda i, s: (s[0], 0, 0, 0)),
            (cotangent, block, lambda i, s: (1 - s[0], 0, 0, 0)),
        ],
        [
            ((rows, width), low, None, None),
            ((rows, width), low, None, None),
            ((rows, 1), wide, None, None),
        ],
        scalars=[core, base, *lengths.reshape(-1)],
    )


def join_kernel(_, keep_send, got_send, keep_own, got_own, send, kept):
    send[...] = (
        (keep_send[...].astype(wide) + got_send[...].astype(wide)).reshape(send.shape).astype(low)
    )
    kept[...] = (
        (keep_own[...].astype(wide) + got_own[...].astype(wide)).reshape(kept.shape).astype(low)
    )


def join(keep, received, outer, bit):
    rows, columns = keep.shape
    inner = rows // (2 * outer)
    view = (outer, 2, inner, columns)
    block = (outer, 1, inner, columns)
    keep, received = keep.reshape(view), received.reshape(view)

    def send_place(i, s):
        return (0, 1 - s[0], 0, 0)

    def own_place(i, s):
        return (0, s[0], 0, 0)

    half = (rows // 2, columns)
    return kernel_call(
        join_kernel,
        [
            (keep, block, send_place),
            (received, block, send_place),
            (keep, block, own_place),
            (received, block, own_place),
        ],
        [(half, low, None, None), (half, low, None, None)],
        scalars=[bit],
    )


def last_kernel(cuts, turn, _, keep, received, *outs):
    total = keep[...].astype(wide) + received[...].astype(wide)
    start = 0
    for cut, out in zip(cuts, outs):
        part = total[:, start : start + cut]
        out[...] = part.T if turn else part
        start += cut


def join_last(keep, received, cuts, turn=False):
    rows = keep.shape[0]
    shapes = [(c, rows) if turn else (rows, c) for c in cuts]
    return kernel_call(
        functools.partial(last_kernel, tuple(cuts), turn),
        [whole(keep), whole(received)],
        [(s, wide, None, None) for s in shapes],
    )
lanes = 128


def grad_kernel(blocks, pairs, has_add, select, *refs):
    del select
    out = refs[-1]
    add = refs[-2] if has_add else None
    start = 0
    refs = list(refs)
    for group in pairs:
        total = None
        for _ in range(group):
            lefts = [refs.pop(0)[...] for _ in range(blocks)]
            left = lefts[0] if blocks == 1 else jnp.concatenate(lefts, axis=1)
            term = matmul_tn(left, refs.pop(0)[...])
            total = term if total is None else total + term
        stop = start + total.shape[1]
        if has_add:
            total = total + add[:, start:stop].astype(wide)
        out[:, start:stop] = total.astype(out.dtype)
        start = stop


def weight_grad(groups, shares, columns, bit, mask, block, add=None):
    width = groups[0][0][0].shape[1]
    run = mask * block
    unit = run if run % lanes == 0 else width // 2
    count = width // 2 // unit
    select = jnp.stack([bit, columns]).astype(jnp.int32)
    operands, specs = [], []

    def left_map(k):
        return lambda i, chosen: (0, 2 * k + chosen[0])

    for group, share in zip(groups, shares):
        for left, right in group:
            rows = left.shape[0]
            if run % lanes:
                view = left.reshape(rows, width // (2 * run), 2, run)
                picked = lax.dynamic_index_in_dim(view, bit, 2, keepdims=False)
                operands.append(picked.reshape(rows, width // 2))
                specs.append(pl.BlockSpec((rows, width // 2), lambda i, chosen: (0, 0)))
            else:
                for k in range(count):
                    operands.append(left)
                    specs.append(pl.BlockSpec((rows, unit), left_map(k)))
            operands.append(right)
            specs.append(pl.BlockSpec((rows, share), lambda i, chosen: (0, chosen[1])))
    total = sum(shares)
    if add is not None:
        operands.append(add)
        specs.append(pl.BlockSpec((width // 2, total), lambda i, chosen: (0, 0)))
    return pl.pallas_call(
        functools.partial(grad_kernel, count, tuple(len(g) for g in groups), add is not None),
        grid_spec=pltpu.PrefetchScalarGridSpec(
            num_scalar_prefetch=1,
            grid=(1,),
            in_specs=specs,
            out_specs=pl.BlockSpec((width // 2, total), lambda i, chosen: (0, 0)),
        ),
        out_shape=jax.ShapeDtypeStruct((width // 2, total), low),
        compiler_params=pltpu.CompilerParams(vmem_limit_bytes=vmem_bytes),
    )(select, *operands)


def expand(normed, gate_weight, up_weight):
    gate = matmul(normed, gate_weight)
    up = matmul(normed, up_weight)
    sigmoid = jax.nn.sigmoid(gate)
    return (gate * sigmoid * up).astype(low), gate, up


def back(out_low, down_weight, gate, up):
    sigmoid = jax.nn.sigmoid(gate)
    act_grad = matmul_nt(out_low, down_weight)
    gate_grad = act_grad * up * sigmoid * (1.0 + gate * (1.0 - sigmoid))
    return gate_grad.astype(low), (act_grad * gate * sigmoid).astype(low)


def two_terms(gate_grad, up_grad, gate_weight, up_weight):
    return matmul_nt(gate_grad, gate_weight) + matmul_nt(up_grad, up_weight)


def conv_forward(product, before, taps):
    groups, length, width = product.shape
    extended = jnp.concatenate([before, product], axis=1).astype(wide)
    terms = [extended[:, k : k + length] for k in range(taps.shape[0])]
    return terms, sum(taps[k] * term for k, term in enumerate(terms))


def to_residual(first, second, residual, out_low, gain, out_weight, c_part):
    grad = first.astype(wide) + second.astype(wide)
    scaled, scale = normed(residual, None)
    grad_norm2 = jnp.sum(grad * scaled, axis=0, keepdims=True)
    weighted = grad * gain
    residual_grad = out_low.astype(wide) + scale * (
        weighted - scaled * jnp.mean(weighted * scaled, axis=-1, keepdims=True)
    )
    residual_low = residual_grad.astype(low)
    gated_grad = matmul_nt(residual_low, out_weight)
    conv_grad = (gated_grad * c_part.astype(wide)).astype(low)
    return residual_grad, residual_low, gated_grad, conv_grad, grad_norm2


def to_projected(conv_grad, after, gated_grad, product, before, b_part, x_part, taps):
    terms, conv_out = conv_forward(product, before, taps)
    groups, length, width = product.shape
    rows = groups * length
    count = taps.shape[0]
    ext_back = jnp.concatenate([conv_grad.reshape(product.shape), after], axis=1).astype(wide)
    grad_conv = jnp.stack([jnp.sum(ext_back[:, :length] * term, axis=(0, 1)) for term in terms])
    product_grad = sum(
        taps[k] * ext_back[:, count - 1 - k : count - 1 - k + length] for k in range(count)
    ).reshape(rows, width)
    projected_grad = jnp.concatenate(
        [
            product_grad * x_part.astype(wide),
            gated_grad * conv_out.reshape(rows, width),
            product_grad * b_part.astype(wide),
        ],
        axis=-1,
    ).astype(low)
    return projected_grad, grad_conv


def to_tokens(projected_grad, in_weight, inputs, residual_grad, gain):
    grad = matmul_nt(projected_grad, in_weight)
    scaled, scale = normed(inputs.astype(wide).reshape(grad.shape), None)
    grad_norm1 = jnp.sum(grad * scaled, axis=0, keepdims=True)
    weighted = grad * gain
    input_grad = residual_grad + scale * (
        weighted - scaled * jnp.mean(weighted * scaled, axis=-1, keepdims=True)
    )
    return input_grad.astype(low), grad_norm1


class Order:
    def __init__(self):
        self.last = None

    def __call__(self, task, *values):
        if self.last is not None:
            values, _ = lax.optimization_barrier((values, self.last))
        result = task(*values)
        self.last = result
        return result


class Spread:
    def __init__(self, masks, share):
        self.masks = masks
        self.share = share
        self.index = lax.axis_index("seq")

    def bit(self, mask):
        return (self.index // mask) % 2

    def local(self, groups, shares, columns, kept, add=None):
        mask = self.masks[0]
        mine = self.bit(mask)
        bit = mine if kept else 1 - mine
        return weight_grad(groups, shares, columns, bit, mask, self.share, add)

    def join(self, step, keep, received):
        gone = self.masks[: step + 1]
        left = [m for m in sorted(self.masks, reverse=True) if m not in gone]
        mask = self.masks[step + 1]
        return join(keep, received, 2 ** left.index(mask), self.bit(mask))

    def rest(self, step, cuts, turn, keep, received):
        while step + 1 < len(self.masks):
            send, keep = self.join(step, keep, received)
            step += 1
            received = self.move(step, send)
        return join_last(keep, received, cuts, turn)

    def move(self, step, send):
        return swap(send, "seq", self.masks[step])


class Vectors:
    def __init__(self, share):
        self.share = share
        self.count = lax.axis_size("seq")
        self.index = lax.axis_index("seq")

    def start(self, *vectors):
        total = jnp.concatenate(vectors, axis=0)
        return total.reshape(total.shape[0], self.count, self.share).transpose(1, 0, 2)

    def halve(self, kept, received):
        total = kept + received
        half = total.shape[0] // 2
        mine = (self.index // half) % 2
        view = total.reshape((2, half) + total.shape[1:])
        return pick(view, 0, 1 - mine), pick(view, 0, mine)

    def move(self, sent):
        return swap(sent, "seq", sent.shape[0])

    def end(self, kept, received):
        while kept.shape[0] > 1:
            sent, kept = self.halve(kept, received)
            received = self.move(sent)
        return (kept + received)[0]


def over_x(block):
    count = lax.axis_size("tp")
    mask = 2
    while 2 * mask < count:
        block = (block.astype(wide) + swap(block, "tp", mask).astype(wide)).astype(low)
        mask *= 2
    return block, swap(block, "tp", mask)


def body(
    tokens,
    lengths,
    norm1_gain,
    in_weight,
    conv_weight,
    out_weight,
    norm2_gain,
    gate_weight,
    up_weight,
    down_weight,
    cotangent,
):
    micro_count, seq_count, shard_length, width = tokens.shape
    tp_count, tp_index = lax.axis_size("tp"), lax.axis_index("tp")
    seq_total, seq_index = lax.axis_size("seq"), lax.axis_index("seq")
    core = tp_index % 2
    own_micro = micro_count // 2
    groups = own_micro * seq_count
    in_share = in_weight.shape[1] // tp_count
    out_share = width // tp_count
    share = width // seq_total
    hidden = gate_weight.shape[1]
    masks = []
    mask = 1
    while mask < seq_total:
        masks.append(mask)
        mask *= 2
    spread = Spread(masks, share)
    vectors = Vectors(share)
    order = Order()
    none = jnp.int32(0)
    taps = conv_weight.astype(wide)

    normed_one, product, b_part, x_part = front(tokens, core, own_micro, norm1_gain, in_weight)
    edge = product.reshape(groups, shard_length, width)[:, shard_length - 2 :]
    before = shift_blocks(edge, 1)
    normed_one, edge = lax.optimization_barrier((normed_one, edge))
    low_own, low_other, own_mask = masked(
        cotangent, lengths, core, seq_index * shard_length, own_micro
    )
    c_part = c_columns(normed_one, in_weight)
    gated_out, residual, normed_own = middle(
        tokens, core, own_micro, product, before, c_part, taps, out_weight, norm2_gain
    )
    normed_other = swap(normed_own, "tp", 1)

    def grad_part(kept):
        return lambda *pairs: spread.local([[pairs[:2], pairs[2:]]], [hidden], none, kept)

    def joined(step):
        return functools.partial(spread.join, step)

    def final(cuts, turn=False):
        return functools.partial(spread.rest, 2, cuts, turn)

    act_own, gate_own, up_own = order(expand, normed_own, gate_weight, up_weight)
    act_other, gate_other, up_other = order(expand, normed_other, gate_weight, up_weight)
    down = (low_own, act_own, low_other, act_other)
    down_moved = spread.move(0, order(grad_part(False), *down))
    gate_grad_other, up_grad_other = order(back, low_other, down_weight, gate_other, up_other)
    two_other = order(
        lambda *v: two_terms(*v, gate_weight, up_weight).astype(low), gate_grad_other, up_grad_other
    )
    two_moved = swap(two_other, "tp", 1)
    ffn_other = order(lambda a: matmul(a, down_weight).astype(low), act_other)
    ffn_moved = swap(ffn_other, "tp", 1)
    gate_grad_own, up_grad_own = order(back, low_own, down_weight, gate_own, up_own)
    two_own = order(lambda *v: two_terms(*v, gate_weight, up_weight), gate_grad_own, up_grad_own)
    ffn_own = order(lambda a: matmul(a, down_weight), act_own)
    two_half = order(lambda a, c: (a + c.astype(wide)).astype(low), two_own, two_moved)
    two_first, two_second = over_x(two_half)
    gate = (normed_own, gate_grad_own, normed_other, gate_grad_other)
    up = (normed_own, up_grad_own, normed_other, up_grad_other)
    down_kept = order(grad_part(True), *down)
    gate_moved = spread.move(0, order(grad_part(False), *gate))
    down_sent, down_kept = order(joined(0), down_kept, down_moved)
    down_moved = spread.move(1, down_sent)
    ffn_half = order(lambda a, c: (a + c.astype(wide)).astype(low), ffn_own, ffn_moved)
    gate_kept = order(grad_part(True), *gate)

    up_moved = spread.move(0, order(grad_part(False), *up))

    residual_grad, residual_low, gated_grad, conv_grad, grad_norm2 = order(
        lambda *v: to_residual(*v, norm2_gain, out_weight, c_part),
        two_first,
        two_second,
        residual,
        low_own,
    )
    after = shift_blocks(conv_grad.reshape(groups, shard_length, width)[:, :2], -1)
    ffn_half, _ = lax.optimization_barrier((ffn_half, two_second))
    ffn_first, ffn_second = over_x(ffn_half)
    gate_sent, gate_kept = order(joined(0), gate_kept, gate_moved)
    gate_moved = spread.move(1, gate_sent)
    down_sent, down_kept = order(joined(1), down_kept, down_moved)
    down_moved = spread.move(2, down_sent)
    view = product.reshape(groups, shard_length, width)
    projected_grad, grad_conv = order(
        lambda *v: to_projected(*v, taps),
        conv_grad,
        after,
        gated_grad,
        view,
        before,
        b_part,
        x_part,
    )
    shares = [in_share, out_share]
    peer = tp_index + 1 - 2 * core

    def tail_part(columns, kept):
        def part(a, b, c, d, add=None):
            return spread.local([[(a, b)], [(c, d)]], shares, columns, kept, add)

        return part

    tail = (normed_one, projected_grad, gated_out, residual_low)
    tail_sent = swap(order(tail_part(peer, False), *tail), "tp", 1)
    tail_kept = swap(order(tail_part(peer, True), *tail), "tp", 1)
    inputs = lax.dynamic_slice_in_dim(tokens, core * own_micro, own_micro, 0)
    input_grad, grad_norm1 = order(
        lambda a, b, c: to_tokens(a, in_weight, b, c, norm1_gain),
        projected_grad,
        inputs,
        residual_grad,
    )
    input_moved = swap(input_grad, "tp", 1)
    gate_sent, gate_kept = order(joined(1), gate_kept, gate_moved)
    gate_moved = spread.move(2, gate_sent)
    vector_kept = order(vectors.start, grad_norm1, grad_norm2, grad_conv)
    vector_moved = swap(vector_kept, "tp", 1)
    up_kept = order(grad_part(True), *up)
    mixed_own = order(
        lambda r, a, b: ((r + (a.astype(wide) + b.astype(wide))) * own_mask).astype(low),
        residual,
        ffn_first,
        ffn_second,
    )
    mixed_moved = swap(mixed_own, "tp", 1)
    up_sent, up_kept = order(joined(0), up_kept, up_moved)
    up_moved = spread.move(1, up_sent)
    (grad_down,) = order(final([hidden], True), down_kept, down_moved)
    vector_sent, vector_kept = order(vectors.halve, vector_kept, vector_moved)
    tail_sent = order(tail_part(tp_index, False), *tail, tail_sent)
    vector_moved = vectors.move(vector_sent)
    tail_moved = spread.move(0, tail_sent)
    tail_kept = order(tail_part(tp_index, True), *tail, tail_kept)

    def both(own, other):
        return assemble(own, other, core, own_micro, tokens.shape)

    tokens_grad = order(both, input_grad, input_moved)
    mixed = order(both, mixed_own, mixed_moved)
    up_sent, up_kept = order(joined(1), up_kept, up_moved)
    up_moved = spread.move(2, up_sent)
    (grad_gate,) = order(final([hidden]), gate_kept, gate_moved)
    tail_sent, tail_kept = order(joined(0), tail_kept, tail_moved)
    vector_sent, vector_kept = order(vectors.halve, vector_kept, vector_moved)
    vector_moved = vectors.move(vector_sent)
    tail_moved = spread.move(1, tail_sent)
    tail_sent, tail_kept = order(joined(1), tail_kept, tail_moved)
    vector_sent, vector_kept = order(vectors.halve, vector_kept, vector_moved)
    vector_moved = vectors.move(vector_sent)
    tail_moved = spread.move(2, tail_sent)
    (grad_up,) = order(final([hidden]), up_kept, up_moved)
    grad_in, grad_out = order(final(shares), tail_kept, tail_moved)
    small = order(vectors.end, vector_kept, vector_moved)
    return (
        mixed,
        tokens_grad,
        small[0],
        grad_in,
        small[2:],
        grad_out,
        small[1],
        grad_gate,
        grad_up,
        grad_down,
    )


def solution(mesh):
    placed = (
        P(None, None, "seq", None),
        P(),
        P(),
        P(),
        P(),
        P(),
        P(),
        P(None, "tp"),
        P(None, "tp"),
        P("tp", None),
        P(None, None, "seq", None),
    )
    return jax.shard_map(
        body,
        mesh=mesh,
        in_specs=placed,
        out_specs=(
            P(None, None, "seq", None),
            P(None, None, "seq", None),
            P("seq"),
            P("seq", "tp"),
            P(None, "seq"),
            P("seq", "tp"),
            P("seq"),
            P("seq", "tp"),
            P("seq", "tp"),
            P("tp", "seq"),
        ),
        check_vma=False,
    )
```

```python
import functools

import jax
import jax.numpy as jnp
from jax import lax
from jax.experimental import pallas as pl
from jax.experimental.pallas import tpu as pltpu
from jax.sharding import PartitionSpec as P

eps = 1e-05
wide = jnp.float32
low = jnp.bfloat16


def shift_blocks(block, distance):
    devices = range(lax.axis_size("seq"))
    route = [(i - distance, i) for i in devices if i - distance in devices]
    return lax.ppermute(block, "seq", route)


def swap(block, axis, mask):
    return lax.ppermute(block, axis, [(i, i ^ mask) for i in range(lax.axis_size(axis))])


def matmul(left, right):
    return jnp.dot(left, right, preferred_element_type=wide)


def matmul_nt(left, right):
    return lax.dot_general(left, right, (((1,), (1,)), ((), ())), preferred_element_type=wide)


def matmul_tn(left, right):
    return lax.dot_general(left, right, (((0,), (0,)), ((), ())), preferred_element_type=wide)


def pick(array, axis, index):
    return lax.dynamic_index_in_dim(array, index, axis, keepdims=False)


vmem_bytes = 20 * 2**20


def kernel_call(kernel, inputs, outputs, grid=(1,), scalars=None, scratch=(), room=vmem_bytes):
    scalars = jnp.zeros((1,), jnp.int32) if scalars is None else jnp.stack(scalars)

    def spec(shape, block, place):
        if block is None:
            zeros = (0,) * len(shape)
            return pl.BlockSpec(tuple(shape), lambda *_: zeros)
        return pl.BlockSpec(block, place)

    return pl.pallas_call(
        kernel,
        grid_spec=pltpu.PrefetchScalarGridSpec(
            num_scalar_prefetch=1,
            grid=grid,
            in_specs=[spec(a.shape, b, m) for a, b, m in inputs],
            out_specs=[spec(s, b, m) for s, _, b, m in outputs],
            scratch_shapes=list(scratch),
        ),
        out_shape=[jax.ShapeDtypeStruct(s, d) for s, d, _, _ in outputs],
        compiler_params=pltpu.CompilerParams(vmem_limit_bytes=room),
    )(scalars.astype(jnp.int32), *[a for a, _, _ in inputs])


def whole(array):
    return (array, None, None)


def normed(values, gain):
    scale = lax.rsqrt(jnp.mean(values * values, axis=-1, keepdims=True) + eps)
    return values * scale, scale


def front_kernel(_, tokens, gain, b_weight, x_weight, normed_one, product, b_part, x_part):
    @pl.when(pl.program_id(0) == 0)
    def _():
        inputs = tokens[...].astype(wide).reshape(normed_one.shape)
        scaled, _ = normed(inputs, None)
        normed_one[...] = (scaled * gain[...]).astype(low)

    b = matmul(normed_one[...], b_weight[...])
    x = matmul(normed_one[...], x_weight[...])
    product[...] = (b * x).astype(low)
    b_part[...] = b.astype(low)
    x_part[...] = x.astype(low)


def front(tokens, core, own_micro, gain, in_weight):
    _, seq_count, length, width = tokens.shape
    rows = own_micro * seq_count * length
    cut = width // 2
    column = ((rows, width), low, (rows, cut), lambda j, s: (0, j))
    return kernel_call(
        front_kernel,
        [
            (tokens, (own_micro, seq_count, length, width), lambda j, s: (s[0], 0, 0, 0)),
            whole(gain[None]),
            (in_weight, (width, cut), lambda j, s: (0, j)),
            (in_weight, (width, cut), lambda j, s: (0, 4 + j)),
        ],
        [((rows, width), low, None, None), column, column, column],
        grid=(2,),
        scalars=[core],
        room=60 * 2**20,
    )


def c_kernel(_, normed_one, weight, out):
    out[...] = matmul(normed_one[...], weight[...]).astype(low)


def c_columns(normed_one, in_weight):
    rows, width = normed_one.shape
    cut = width // 2
    return kernel_call(
        c_kernel,
        [whole(normed_one), (in_weight, (width, cut), lambda j, s: (0, 2 + j))],
        [((rows, width), low, (rows, cut), lambda j, s: (0, j))],
        grid=(2,),
        room=60 * 2**20,
    )[0]


def shifted_down(block, before, distance):
    moved = pltpu.roll(block, distance, 0)
    row = lax.broadcasted_iota(jnp.int32, block.shape, 0)
    for i in range(distance):
        moved = jnp.where(row == i, before[2 - distance + i : 3 - distance + i], moved)
    return moved


def middle_kernel(
    _, tokens, product, before, c_part, taps, out_weight, gain, gated, residual, normed_two
):
    step = pl.program_id(0)
    groups, length, _ = product.shape

    @pl.when(step == 0)
    def _():
        residual[...] = tokens[...].astype(wide).reshape(residual.shape)

    for g in range(groups):
        block = product[g].astype(wide)
        ahead = before[g].astype(wide)
        conv_out = (
            taps[0:1] * shifted_down(block, ahead, 2)
            + taps[1:2] * shifted_down(block, ahead, 1)
            + taps[2:3] * block
        )
        rows = slice(g * length, (g + 1) * length)
        gated[rows] = (c_part[rows].astype(wide) * conv_out).astype(low)
    residual[...] += matmul(gated[...], out_weight[...])

    @pl.when(step == pl.num_programs(0) - 1)
    def _():
        scaled, _ = normed(residual[...], None)
        normed_two[...] = (scaled * gain[...]).astype(low)


def middle(tokens, core, own_micro, product, before, c_part, taps, out_weight, gain):
    _, seq_count, length, width = tokens.shape
    groups = own_micro * seq_count
    rows = groups * length
    cut = width
    return kernel_call(
        middle_kernel,
        [
            (tokens, (own_micro, seq_count, length, width), lambda k, s: (s[0], 0, 0, 0)),
            (product.reshape(groups, length, width), (groups, length, cut), lambda k, s: (0, 0, k)),
            (before, (groups, 2, cut), lambda k, s: (0, 0, k)),
            (c_part, (rows, cut), lambda k, s: (0, k)),
            (taps, (taps.shape[0], cut), lambda k, s: (0, k)),
            (out_weight, (cut, width), lambda k, s: (k, 0)),
            whole(gain[None]),
        ],
        [
            ((rows, width), low, (rows, cut), lambda k, s: (0, k)),
            ((rows, width), wide, None, None),
            ((rows, width), low, None, None),
        ],
        grid=(1,),
        scalars=[core],
    )


def assemble_kernel(_, own, other, out):
    @pl.when(pl.program_id(0) == 0)
    def _():
        out[...] = own[...].reshape(out.shape)

    @pl.when(pl.program_id(0) == 1)
    def _():
        out[...] = other[...].reshape(out.shape)


def assemble(own, other, core, own_micro, shape):
    block = (own_micro,) + tuple(shape[1:])
    return kernel_call(
        assemble_kernel,
        [whole(own), whole(other)],
        [(tuple(shape), low, block, lambda i, s: (jnp.where(i == 0, s[0], 1 - s[0]), 0, 0, 0))],
        grid=(2,),
        scalars=[core],
    )[0]


def mask_kernel(scalars, own, other, own_low, other_low, mask):
    micros, seqs, length, width = own.shape
    core, base = scalars[0], scalars[1]
    position = base + lax.broadcasted_iota(jnp.int32, (length, 1), 0)
    for source, which, out in ((own, core, own_low), (other, 1 - core, other_low)):
        for m in range(micros):
            for n in range(seqs):
                limit = scalars[2 + (which * micros + m) * seqs + n]
                keep = (position < limit).astype(wide)
                rows = slice((m * seqs + n) * length, (m * seqs + n + 1) * length)
                out[rows] = (source[m, n].astype(wide) * keep).astype(low)
                if out is own_low:
                    mask[rows] = keep


def masked(cotangent, lengths, core, base, own_micro):
    _, seq_count, length, width = cotangent.shape
    rows = own_micro * seq_count * length
    block = (own_micro, seq_count, length, width)
    return kernel_call(
        mask_kernel,
        [
            (cotangent, block, lambda i, s: (s[0], 0, 0, 0)),
            (cotangent, block, lambda i, s: (1 - s[0], 0, 0, 0)),
        ],
        [
            ((rows, width), low, None, None),
            ((rows, width), low, None, None),
            ((rows, 1), wide, None, None),
        ],
        scalars=[core, base, *lengths.reshape(-1)],
    )


def join_kernel(_, keep_send, got_send, keep_own, got_own, send, kept):
    send[...] = (
        (keep_send[...].astype(wide) + got_send[...].astype(wide)).reshape(send.shape).astype(low)
    )
    kept[...] = (
        (keep_own[...].astype(wide) + got_own[...].astype(wide)).reshape(kept.shape).astype(low)
    )


def join(keep, received, outer, bit):
    rows, columns = keep.shape
    inner = rows // (2 * outer)
    view = (outer, 2, inner, columns)
    block = (outer, 1, inner, columns)
    keep, received = keep.reshape(view), received.reshape(view)

    def send_place(i, s):
        return (0, 1 - s[0], 0, 0)

    def own_place(i, s):
        return (0, s[0], 0, 0)

    half = (rows // 2, columns)
    return kernel_call(
        join_kernel,
        [
            (keep, block, send_place),
            (received, block, send_place),
            (keep, block, own_place),
            (received, block, own_place),
        ],
        [(half, low, None, None), (half, low, None, None)],
        scalars=[bit],
    )


def last_kernel(cuts, turn, _, keep, received, *outs):
    total = keep[...].astype(wide) + received[...].astype(wide)
    start = 0
    for cut, out in zip(cuts, outs):
        part = total[:, start : start + cut]
        out[...] = part.T if turn else part
        start += cut


def join_last(keep, received, cuts, turn=False):
    rows = keep.shape[0]
    shapes = [(c, rows) if turn else (rows, c) for c in cuts]
    return kernel_call(
        functools.partial(last_kernel, tuple(cuts), turn),
        [whole(keep), whole(received)],
        [(s, wide, None, None) for s in shapes],
    )
lanes = 128


def grad_kernel(blocks, pairs, has_add, select, *refs):
    del select
    out = refs[-1]
    add = refs[-2] if has_add else None
    start = 0
    refs = list(refs)
    for group in pairs:
        total = None
        for _ in range(group):
            lefts = [refs.pop(0)[...] for _ in range(blocks)]
            left = lefts[0] if blocks == 1 else jnp.concatenate(lefts, axis=1)
            term = matmul_tn(left, refs.pop(0)[...])
            total = term if total is None else total + term
        stop = start + total.shape[1]
        if has_add:
            total = total + add[:, start:stop].astype(wide)
        out[:, start:stop] = total.astype(out.dtype)
        start = stop


def weight_grad(groups, shares, columns, bit, mask, block, add=None):
    width = groups[0][0][0].shape[1]
    run = mask * block
    unit = run if run % lanes == 0 else width // 2
    count = width // 2 // unit
    select = jnp.stack([bit, columns]).astype(jnp.int32)
    operands, specs = [], []

    def left_map(k):
        return lambda i, chosen: (0, 2 * k + chosen[0])

    for group, share in zip(groups, shares):
        for left, right in group:
            rows = left.shape[0]
            if run % lanes:
                view = left.reshape(rows, width // (2 * run), 2, run)
                picked = lax.dynamic_index_in_dim(view, bit, 2, keepdims=False)
                operands.append(picked.reshape(rows, width // 2))
                specs.append(pl.BlockSpec((rows, width // 2), lambda i, chosen: (0, 0)))
            else:
                for k in range(count):
                    operands.append(left)
                    specs.append(pl.BlockSpec((rows, unit), left_map(k)))
            operands.append(right)
            specs.append(pl.BlockSpec((rows, share), lambda i, chosen: (0, chosen[1])))
    total = sum(shares)
    if add is not None:
        operands.append(add)
        specs.append(pl.BlockSpec((width // 2, total), lambda i, chosen: (0, 0)))
    return pl.pallas_call(
        functools.partial(grad_kernel, count, tuple(len(g) for g in groups), add is not None),
        grid_spec=pltpu.PrefetchScalarGridSpec(
            num_scalar_prefetch=1,
            grid=(1,),
            in_specs=specs,
            out_specs=pl.BlockSpec((width // 2, total), lambda i, chosen: (0, 0)),
        ),
        out_shape=jax.ShapeDtypeStruct((width // 2, total), low),
        compiler_params=pltpu.CompilerParams(vmem_limit_bytes=vmem_bytes),
    )(select, *operands)


def expand(normed, gate_weight, up_weight):
    gate = matmul(normed, gate_weight)
    up = matmul(normed, up_weight)
    sigmoid = jax.nn.sigmoid(gate)
    return (gate * sigmoid * up).astype(low), gate, up


def back(out_low, down_weight, gate, up):
    sigmoid = jax.nn.sigmoid(gate)
    act_grad = matmul_nt(out_low, down_weight)
    gate_grad = act_grad * up * sigmoid * (1.0 + gate * (1.0 - sigmoid))
    return gate_grad.astype(low), (act_grad * gate * sigmoid).astype(low)


def two_terms(gate_grad, up_grad, gate_weight, up_weight):
    return matmul_nt(gate_grad, gate_weight) + matmul_nt(up_grad, up_weight)


def conv_forward(product, before, taps):
    groups, length, width = product.shape
    extended = jnp.concatenate([before, product], axis=1).astype(wide)
    terms = [extended[:, k : k + length] for k in range(taps.shape[0])]
    return terms, sum(taps[k] * term for k, term in enumerate(terms))


def to_residual(first, second, residual, out_low, gain, out_weight, c_part):
    grad = first.astype(wide) + second.astype(wide)
    scaled, scale = normed(residual, None)
    grad_norm2 = jnp.sum(grad * scaled, axis=0, keepdims=True)
    weighted = grad * gain
    residual_grad = out_low.astype(wide) + scale * (
        weighted - scaled * jnp.mean(weighted * scaled, axis=-1, keepdims=True)
    )
    residual_low = residual_grad.astype(low)
    gated_grad = matmul_nt(residual_low, out_weight)
    conv_grad = (gated_grad * c_part.astype(wide)).astype(low)
    return residual_grad, residual_low, gated_grad, conv_grad, grad_norm2


def to_projected(conv_grad, after, gated_grad, product, before, b_part, x_part, taps):
    terms, conv_out = conv_forward(product, before, taps)
    groups, length, width = product.shape
    rows = groups * length
    count = taps.shape[0]
    ext_back = jnp.concatenate([conv_grad.reshape(product.shape), after], axis=1).astype(wide)
    grad_conv = jnp.stack([jnp.sum(ext_back[:, :length] * term, axis=(0, 1)) for term in terms])
    product_grad = sum(
        taps[k] * ext_back[:, count - 1 - k : count - 1 - k + length] for k in range(count)
    ).reshape(rows, width)
    projected_grad = jnp.concatenate(
        [
            product_grad * x_part.astype(wide),
            gated_grad * conv_out.reshape(rows, width),
            product_grad * b_part.astype(wide),
        ],
        axis=-1,
    ).astype(low)
    return projected_grad, grad_conv


def to_tokens(projected_grad, in_weight, inputs, residual_grad, gain):
    grad = matmul_nt(projected_grad, in_weight)
    scaled, scale = normed(inputs.astype(wide).reshape(grad.shape), None)
    grad_norm1 = jnp.sum(grad * scaled, axis=0, keepdims=True)
    weighted = grad * gain
    input_grad = residual_grad + scale * (
        weighted - scaled * jnp.mean(weighted * scaled, axis=-1, keepdims=True)
    )
    return input_grad.astype(low), grad_norm1


class Order:
    def __init__(self):
        self.last = None

    def __call__(self, task, *values):
        if self.last is not None:
            values, _ = lax.optimization_barrier((values, self.last))
        result = task(*values)
        self.last = result
        return result


class Spread:
    def __init__(self, masks, share):
        self.masks = masks
        self.share = share
        self.index = lax.axis_index("seq")

    def bit(self, mask):
        return (self.index // mask) % 2

    def local(self, groups, shares, columns, kept, add=None):
        mask = self.masks[0]
        mine = self.bit(mask)
        bit = mine if kept else 1 - mine
        return weight_grad(groups, shares, columns, bit, mask, self.share, add)

    def join(self, step, keep, received):
        gone = self.masks[: step + 1]
        left = [m for m in sorted(self.masks, reverse=True) if m not in gone]
        mask = self.masks[step + 1]
        return join(keep, received, 2 ** left.index(mask), self.bit(mask))

    def rest(self, step, cuts, turn, keep, received):
        while step + 1 < len(self.masks):
            send, keep = self.join(step, keep, received)
            step += 1
            received = self.move(step, send)
        return join_last(keep, received, cuts, turn)

    def move(self, step, send):
        return swap(send, "seq", self.masks[step])


class Vectors:
    def __init__(self, share):
        self.share = share
        self.count = lax.axis_size("seq")
        self.index = lax.axis_index("seq")

    def start(self, *vectors):
        total = jnp.concatenate(vectors, axis=0)
        return total.reshape(total.shape[0], self.count, self.share).transpose(1, 0, 2)

    def halve(self, kept, received):
        total = kept + received
        half = total.shape[0] // 2
        mine = (self.index // half) % 2
        view = total.reshape((2, half) + total.shape[1:])
        return pick(view, 0, 1 - mine), pick(view, 0, mine)

    def move(self, sent):
        return swap(sent, "seq", sent.shape[0])

    def end(self, kept, received):
        while kept.shape[0] > 1:
            sent, kept = self.halve(kept, received)
            received = self.move(sent)
        return (kept + received)[0]


def over_x(block):
    count = lax.axis_size("tp")
    mask = 2
    while 2 * mask < count:
        block = (block.astype(wide) + swap(block, "tp", mask).astype(wide)).astype(low)
        mask *= 2
    return block, swap(block, "tp", mask)


def body(
    tokens,
    lengths,
    norm1_gain,
    in_weight,
    conv_weight,
    out_weight,
    norm2_gain,
    gate_weight,
    up_weight,
    down_weight,
    cotangent,
):
    micro_count, seq_count, shard_length, width = tokens.shape
    tp_count, tp_index = lax.axis_size("tp"), lax.axis_index("tp")
    seq_total, seq_index = lax.axis_size("seq"), lax.axis_index("seq")
    core = tp_index % 2
    own_micro = micro_count // 2
    groups = own_micro * seq_count
    in_share = in_weight.shape[1] // tp_count
    out_share = width // tp_count
    share = width // seq_total
    hidden = gate_weight.shape[1]
    masks = []
    mask = 1
    while mask < seq_total:
        masks.append(mask)
        mask *= 2
    spread = Spread(masks, share)
    vectors = Vectors(share)
    order = Order()
    none = jnp.int32(0)
    taps = conv_weight.astype(wide)

    normed_one, product, b_part, x_part = front(tokens, core, own_micro, norm1_gain, in_weight)
    edge = product.reshape(groups, shard_length, width)[:, shard_length - 2 :]
    before = shift_blocks(edge, 1)
    normed_one, edge = lax.optimization_barrier((normed_one, edge))
    low_own, low_other, own_mask = masked(
        cotangent, lengths, core, seq_index * shard_length, own_micro
    )
    c_part = c_columns(normed_one, in_weight)
    gated_out, residual, normed_own = middle(
        tokens, core, own_micro, product, before, c_part, taps, out_weight, norm2_gain
    )
    normed_other = swap(normed_own, "tp", 1)

    def grad_part(kept):
        return lambda *pairs: spread.local([[pairs[:2], pairs[2:]]], [hidden], none, kept)

    def joined(step):
        return functools.partial(spread.join, step)

    def final(cuts, turn=False):
        return functools.partial(spread.rest, 2, cuts, turn)

    act_own, gate_own, up_own = order(expand, normed_own, gate_weight, up_weight)
    act_other, gate_other, up_other = order(expand, normed_other, gate_weight, up_weight)
    down = (low_own, act_own, low_other, act_other)
    down_moved = spread.move(0, order(grad_part(False), *down))
    gate_grad_other, up_grad_other = order(back, low_other, down_weight, gate_other, up_other)
    two_other = order(
        lambda *v: two_terms(*v, gate_weight, up_weight).astype(low), gate_grad_other, up_grad_other
    )
    two_moved = swap(two_other, "tp", 1)
    ffn_other = order(lambda a: matmul(a, down_weight).astype(low), act_other)
    ffn_moved = swap(ffn_other, "tp", 1)
    gate_grad_own, up_grad_own = order(back, low_own, down_weight, gate_own, up_own)
    two_own = order(lambda *v: two_terms(*v, gate_weight, up_weight), gate_grad_own, up_grad_own)
    ffn_own = order(lambda a: matmul(a, down_weight), act_own)
    two_half = order(lambda a, c: (a + c.astype(wide)).astype(low), two_own, two_moved)
    two_first, two_second = over_x(two_half)
    gate = (normed_own, gate_grad_own, normed_other, gate_grad_other)
    up = (normed_own, up_grad_own, normed_other, up_grad_other)
    down_kept = order(grad_part(True), *down)
    gate_moved = spread.move(0, order(grad_part(False), *gate))
    down_sent, down_kept = order(joined(0), down_kept, down_moved)
    down_moved = spread.move(1, down_sent)
    ffn_half = order(lambda a, c: (a + c.astype(wide)).astype(low), ffn_own, ffn_moved)
    gate_kept = order(grad_part(True), *gate)

    up_moved = spread.move(0, order(grad_part(False), *up))

    residual_grad, residual_low, gated_grad, conv_grad, grad_norm2 = order(
        lambda *v: to_residual(*v, norm2_gain, out_weight, c_part),
        two_first,
        two_second,
        residual,
        low_own,
    )
    after = shift_blocks(conv_grad.reshape(groups, shard_length, width)[:, :2], -1)
    ffn_half, _ = lax.optimization_barrier((ffn_half, two_second))
    ffn_first, ffn_second = over_x(ffn_half)
    gate_sent, gate_kept = order(joined(0), gate_kept, gate_moved)
    gate_moved = spread.move(1, gate_sent)
    down_sent, down_kept = order(joined(1), down_kept, down_moved)
    down_moved = spread.move(2, down_sent)
    view = product.reshape(groups, shard_length, width)
    projected_grad, grad_conv = order(
        lambda *v: to_projected(*v, taps),
        conv_grad,
        after,
        gated_grad,
        view,
        before,
        b_part,
        x_part,
    )
    shares = [in_share, out_share]
    peer = tp_index + 1 - 2 * core

    def tail_part(columns, kept):
        def part(a, b, c, d, add=None):
            return spread.local([[(a, b)], [(c, d)]], shares, columns, kept, add)

        return part

    tail = (normed_one, projected_grad, gated_out, residual_low)
    tail_sent = swap(order(tail_part(peer, False), *tail), "tp", 1)
    tail_kept = swap(order(tail_part(peer, True), *tail), "tp", 1)
    inputs = lax.dynamic_slice_in_dim(tokens, core * own_micro, own_micro, 0)
    input_grad, grad_norm1 = order(
        lambda a, b, c: to_tokens(a, in_weight, b, c, norm1_gain),
        projected_grad,
        inputs,
        residual_grad,
    )
    input_moved = swap(input_grad, "tp", 1)
    gate_sent, gate_kept = order(joined(1), gate_kept, gate_moved)
    gate_moved = spread.move(2, gate_sent)
    vector_kept = order(vectors.start, grad_norm1, grad_norm2, grad_conv)
    vector_moved = swap(vector_kept, "tp", 1)
    up_kept = order(grad_part(True), *up)
    mixed_own = order(
        lambda r, a, b: ((r + (a.astype(wide) + b.astype(wide))) * own_mask).astype(low),
        residual,
        ffn_first,
        ffn_second,
    )
    mixed_moved = swap(mixed_own, "tp", 1)
    up_sent, up_kept = order(joined(0), up_kept, up_moved)
    up_moved = spread.move(1, up_sent)
    (grad_down,) = order(final([hidden], True), down_kept, down_moved)
    vector_sent, vector_kept = order(vectors.halve, vector_kept, vector_moved)
    tail_sent = order(tail_part(tp_index, False), *tail, tail_sent)
    vector_moved = vectors.move(vector_sent)
    tail_moved = spread.move(0, tail_sent)
    tail_kept = order(tail_part(tp_index, True), *tail, tail_kept)

    def both(own, other):
        return assemble(own, other, core, own_micro, tokens.shape)

    tokens_grad = order(both, input_grad, input_moved)
    mixed = order(both, mixed_own, mixed_moved)
    up_sent, up_kept = order(joined(1), up_kept, up_moved)
    up_moved = spread.move(2, up_sent)
    (grad_gate,) = order(final([hidden]), gate_kept, gate_moved)
    tail_sent, tail_kept = order(joined(0), tail_kept, tail_moved)
    vector_sent, vector_kept = order(vectors.halve, vector_kept, vector_moved)
    vector_moved = vectors.move(vector_sent)
    tail_moved = spread.move(1, tail_sent)
    tail_sent, tail_kept = order(joined(1), tail_kept, tail_moved)
    vector_sent, vector_kept = order(vectors.halve, vector_kept, vector_moved)
    vector_moved = vectors.move(vector_sent)
    tail_moved = spread.move(2, tail_sent)
    (grad_up,) = order(final([hidden]), up_kept, up_moved)
    grad_in, grad_out = order(final(shares), tail_kept, tail_moved)
    small = order(vectors.end, vector_kept, vector_moved)
    return (
        mixed,
        tokens_grad,
        small[0],
        grad_in,
        small[2:],
        grad_out,
        small[1],
        grad_gate,
        grad_up,
        grad_down,
    )


def solution(mesh):
    placed = (
        P(None, None, "seq", None),
        P(),
        P(),
        P(),
        P(),
        P(),
        P(),
        P(None, "tp"),
        P(None, "tp"),
        P("tp", None),
        P(None, None, "seq", None),
    )
    return jax.shard_map(
        body,
        mesh=mesh,
        in_specs=placed,
        out_specs=(
            P(None, None, "seq", None),
            P(None, None, "seq", None),
            P("seq"),
            P("seq", "tp"),
            P(None, "seq"),
            P("seq", "tp"),
            P("seq"),
            P("seq", "tp"),
            P("seq", "tp"),
            P("tp", "seq"),
        ),
        check_vma=False,
    )
```
